128 devices in a mesh: dp: 16 (over y_lo, z, core), vocab: 8 (over x, y_hi).
Axes of the slice: x: 4, y: 4 (y_hi: 2, y_lo: 2; y = y_hi * 2 + y_lo), z: 4, core: 2. Of those that a mesh axis runs over, the one named last changes fastest.
Arguments:
- student_hidden: bfloat16 [8192, 2560], P(('dp', 'vocab')), may hold values from -6 to 6
- teacher_hidden: bfloat16 [8192, 5120], P(('dp', 'vocab')), may hold values from -6 to 6
- student_head: bfloat16 [9216, 2560], P('vocab'), may hold values from -0.375 to 0.375
- teacher_head: bfloat16 [9216, 5120], P('vocab'), may hold values from -0.25 to 0.25
- sampled_ids: int32 [8192], P('dp'), may hold values from 0 to 9215
Outputs:
- hidden_grad: bfloat16 [8192, 2560], P(('dp', 'vocab'))
- head_grad: bfloat16 [9216, 2560], P(('vocab', 'dp'))
The draws below stay inside these ranges and needn't reach their ends.
All inputs are finite; a program needn't handle non-finite values.
Results may differ from the reference program's by a relative error of at most 0.005.
Values may be sent and summed in bfloat16 or wider, within the bound.
No kernel may reach another device: no remote copies, remote signals or barrier semaphores. Data moves between devices by JAX's collectives and lax.ppermute only.
A program may use at most 192 MiB of HBM per device.

```python
import jax
import jax.numpy as jnp

DS = 2560
DT = 5120
VOCAB = 9216
TOKENS = 8192


def touch_ends(drawn, stream_key, low, top_value):
    spot = [jax.random.randint(jax.random.fold_in(stream_key, axis), (), 0, length) for axis, length in enumerate(drawn.shape)]
    widest = drawn.shape.index(max(drawn.shape))
    neighbour = spot[:widest] + [(spot[widest] + 1) % drawn.shape[widest]] + spot[widest + 1:]
    return drawn.at[tuple(spot)].set(low).at[tuple(neighbour)].set(top_value)


def level_of(rng, dims, cuts, least, top_value):
    level, own = 1.0, jax.random.fold_in(rng, 6)
    for dim, parts in cuts:
        draws = jnp.exp(jax.random.uniform(jax.random.fold_in(own, dim), (parts,), jnp.float32, least / len(cuts), top_value / len(cuts)))
        level = level * jnp.repeat(draws, dims[dim] // parts).reshape([-1 if axis == dim else 1 for axis in range(len(dims))])
    return level


def gaussian(stream_key, extent, width, bound, shards=(), held_as=jnp.bfloat16):
    entries = width * jax.random.normal(stream_key, extent, jnp.float32)
    if shards:
        entries = entries * level_of(stream_key, extent, shards, -0.22, 0.18)
    return jnp.clip(entries, -bound, bound).astype(held_as)


def setup_inputs(seed: int = 0) -> dict:
    key_of = jax.random.split(jax.random.key(seed), 6)
    return {
        "student_hidden": gaussian(key_of[0], (TOKENS, DS), 1.0, 6.0, ((0, 128),)),
        "teacher_hidden": gaussian(key_of[1], (TOKENS, DT), 1.0, 6.0, ((0, 128),)),
        "student_head": gaussian(key_of[2], (VOCAB, DS), (DS // 9) ** -0.5, 0.375, ((0, 8),)),
        "teacher_head": gaussian(key_of[3], (VOCAB, DT), (DT // 9) ** -0.5, 0.25, ((0, 8),)),
        "sampled_ids": touch_ends(jax.random.randint(key_of[4], (TOKENS,), 0, VOCAB), jax.random.fold_in(key_of[4], 1), 0, VOCAB - 1).astype(jnp.int32),
    }


def reference(student_hidden, teacher_hidden, student_head, teacher_head, sampled_ids):
    student_logits = jnp.dot(student_hidden, student_head.T, preferred_element_type=jnp.float32)
    teacher_logits = jnp.dot(teacher_hidden, teacher_head.T, preferred_element_type=jnp.float32)
    student_norm = jnp.log(jnp.sum(jnp.exp(student_logits), axis=1))
    teacher_norm = jnp.log(jnp.sum(jnp.exp(teacher_logits), axis=1))
    picked_student = jnp.take_along_axis(student_logits, sampled_ids[:, None], axis=1)[:, 0]
    picked_teacher = jnp.take_along_axis(teacher_logits, sampled_ids[:, None], axis=1)[:, 0]
    advantage = (picked_teacher - teacher_norm) - (picked_student - student_norm)
    columns = jnp.arange(student_logits.shape[1], dtype=jnp.int32)
    onehot = jnp.where(columns[None, :] == sampled_ids[:, None], 1.0, 0.0)
    probs = jnp.exp(student_logits - student_norm[:, None])
    logit_grad = (advantage[:, None] * (probs - onehot)).astype(jnp.bfloat16)
    hidden_grad = jnp.dot(logit_grad, student_head, preferred_element_type=jnp.float32).astype(jnp.bfloat16)
    head_grad = jnp.dot(logit_grad.T, student_hidden, preferred_element_type=jnp.float32).astype(jnp.bfloat16)
    return hidden_grad, head_grad
```

```python
import functools

import jax
import jax.numpy as jnp
from jax import lax
from jax.experimental import pallas as pl
from jax.experimental.pallas import tpu as pltpu
from jax.sharding import PartitionSpec as P

BF16 = jnp.bfloat16
F32 = jnp.float32
AXES = ("dp", "vocab")

REL = ((0, 0), (-1, 0), (1, 0), (2, 0), (0, 1), (-1, 1), (1, 1), (2, 1))


def pairs(move):
    out = []
    for i in range(128):
        dp, v = i // 8, i % 8
        y_lo, z, core, x, y_hi = dp // 8, (dp // 2) % 4, dp % 2, v // 2, v % 2
        x, y, z, core = move(x, y_hi * 2 + y_lo, z, core)
        x, y, z = x % 4, y % 4, z % 4
        out.append((i, (((y % 2) * 4 + z) * 2 + core) * 8 + x * 2 + y // 2))
    return out


X_UP = pairs(lambda x, y, z, c: (x + 1, y, z, c))
X_DOWN = pairs(lambda x, y, z, c: (x - 1, y, z, c))
X_FAR = pairs(lambda x, y, z, c: (x + 2, y, z, c))
Y_HI = pairs(lambda x, y, z, c: (x, 3 - y, z, c))
Z_UP = pairs(lambda x, y, z, c: (x, y, z + 1, c))
Z_DOWN = pairs(lambda x, y, z, c: (x, y, z - 1, c))
Y_LO = pairs(lambda x, y, z, c: (x, y ^ 1, z, c))
CORE = pairs(lambda x, y, z, c: (x, y, z, 1 - c))


def send(a, to):
    return lax.ppermute(a, AXES, to)


def after(a, *others):
    return lax.optimization_barrier((a, *others))[0]


def params(mib):
    return pltpu.CompilerParams(vmem_limit_bytes=mib * 2**20)


def whole(shape):
    return pl.BlockSpec(shape, lambda *_: (0,) * len(shape))


SMEM = pl.BlockSpec(memory_space=pltpu.SMEM)


def fold(a):
    return jnp.sum(a.reshape(a.shape[0] // 8, 8, a.shape[1]), axis=0)


def add_stats(j, last, logits, ids_ref, base, stats_ref, sums, picks):
    rows = lax.broadcasted_iota(jnp.int32, logits.shape, 0) + (base + j * logits.shape[0])
    some = fold(jnp.exp(logits))
    pick = fold(jnp.where(rows == ids_ref[...], logits, 0.0))

    @pl.when(j == 0)
    def _():
        sums[...] = some
        picks[...] = pick

    @pl.when(j > 0)
    def _():
        sums[...] += some
        picks[...] += pick

    @pl.when(j == last)
    def _():
        stats_ref[...] = jnp.zeros_like(stats_ref)
        stats_ref[0:1, :] = jnp.sum(sums[...], axis=0, keepdims=True)
        stats_ref[1:2, :] = jnp.sum(picks[...], axis=0, keepdims=True)


NT = (((1,), (1,)), ((), ()))
NN = (((1,), (0,)), ((), ()))


def student_kernel(last, pos, ids, own, left, right, near, left_near, right_near, far_a, far_b, far_near_a,
                   far_near_b, head, logits, hidden, stats, sums, picks):
    j = pl.program_id(0)

    @pl.when(j == 0)
    def _():
        halves = [(r[0:32, :], r[32:64, :]) for r in (own, left, right)]
        halves.append((far_a[...], far_b[...]))
        halves += [(r[0:32, :], r[32:64, :]) for r in (near, left_near, right_near)]
        halves.append((far_near_a[...], far_near_b[...]))
        for r in range(8):
            for h in range(2):
                hidden[pl.ds(pl.multiple_of(h * 256 + pos[r] * 32, 32), 32), :] = halves[r][h]

    out = lax.dot_general(head[...], hidden[...], NT, preferred_element_type=F32)
    logits[...] = out
    add_stats(j, last, out, ids, pos[8], stats, sums, picks)


def student_logits(pos, ids, blocks, head, tile=384):
    v, d = head.shape
    return pl.pallas_call(
        functools.partial(student_kernel, v // tile - 1),
        grid=(v // tile,),
        in_specs=[SMEM, whole((1, 512))]
        + [whole(b.shape) for b in blocks]
        + [pl.BlockSpec((tile, d), lambda j: (j, 0))],
        out_specs=[pl.BlockSpec((tile, 512), lambda j: (j, 0)), whole((512, d)), whole((8, 512))],
        out_shape=[
            jax.ShapeDtypeStruct((v, 512), F32),
            jax.ShapeDtypeStruct((512, d), BF16),
            jax.ShapeDtypeStruct((8, 512), F32),
        ],
        scratch_shapes=[pltpu.VMEM((8, 512), F32)] * 2,
        compiler_params=params(40),
        cost_estimate=pl.CostEstimate(flops=2 * v * 512 * d, bytes_accessed=2 * v * d + 8 * 512 * d, transcendentals=v * 512),
    )(pos, ids, *blocks, head)


def teacher_kernel(last, pos, ids, *refs):
    blocks, (head, stats, hidden, sums, picks) = refs[:8], refs[8:]
    j = pl.program_id(0)

    @pl.when(j == 0)
    def _():
        for r in range(8):
            hidden[pl.ds(pl.multiple_of(pos[r] * 32, 32), 32), :] = blocks[r][...]

    out = lax.dot_general(head[...], hidden[...], NT, preferred_element_type=F32)
    add_stats(j, last, out, ids, pos[8], stats, sums, picks)


def teacher_stats(pos, ids, blocks, head, tile=384):
    v, d = head.shape
    return pl.pallas_call(
        functools.partial(teacher_kernel, v // tile - 1),
        grid=(v // tile,),
        in_specs=[SMEM, whole((1, 256))]
        + [whole(b.shape) for b in blocks]
        + [pl.BlockSpec((tile, d), lambda j: (j, 0))],
        out_specs=whole((8, 256)),
        out_shape=jax.ShapeDtypeStruct((8, 256), F32),
        scratch_shapes=[pltpu.VMEM((256, d), BF16)] + [pltpu.VMEM((8, 256), F32)] * 2,
        compiler_params=params(40),
        cost_estimate=pl.CostEstimate(flops=2 * v * 256 * d, bytes_accessed=2 * v * d + 512 * d, transcendentals=v * 256),
    )(pos, ids, *blocks, head)


def hidden_kernel(pos, ids, total, logits, head, own, left, right, near, left_near, right_near, far_a, far_b,
                  far_near, grad_t, product):
    @pl.when(pl.program_id(0) == 0)
    def _():
        norm = jnp.log(total[0:1, :])
        for k in range(9):
            rows = lax.broadcasted_iota(jnp.int32, (128, 512), 0) + (pos[8] + k * 128)
            onehot = jnp.where(rows == ids[...], 1.0, 0.0)
            part = jnp.exp(logits[k * 128:(k + 1) * 128, :] - norm) - onehot
            grad_t[:, k * 128:(k + 1) * 128] = part.T.astype(BF16)

    product[...] = lax.dot_general(grad_t[...], head[...], NN, preferred_element_type=F32)

    def rows_of(r, h):
        return product[pl.ds(pl.multiple_of(h * 256 + pos[r] * 32, 32), 32), :]

    for r, out in ((0, own), (1, left), (2, right), (4, near), (5, left_near), (6, right_near), (7, far_near)):
        for h in range(2):
            out[h * 32:(h + 1) * 32, :] = rows_of(r, h).astype(out.dtype)
    far_a[...] = rows_of(3, 0).astype(far_a.dtype)
    far_b[...] = rows_of(3, 1).astype(far_b.dtype)


def hidden_parts(pos, ids, total, logits, head, tile=512):
    v, d = head.shape
    shapes = [(64, F32)] * 4 + [(64, BF16)] * 2 + [(32, F32)] * 2 + [(64, BF16)]
    return pl.pallas_call(
        hidden_kernel,
        grid=(d // tile,),
        in_specs=[SMEM, whole((1, 512)), whole((8, 512)), whole((v, 512)), pl.BlockSpec((v, tile), lambda j: (0, j))],
        out_specs=[pl.BlockSpec((n, tile), lambda j: (0, j)) for n, _ in shapes],
        out_shape=[jax.ShapeDtypeStruct((n, d), t) for n, t in shapes],
        scratch_shapes=[pltpu.VMEM((512, v), BF16), pltpu.VMEM((512, tile), F32)],
        compiler_params=params(40),
        cost_estimate=pl.CostEstimate(flops=2 * v * 512 * d, bytes_accessed=2 * v * d + 4 * v * 512 + 1500 * d, transcendentals=v * 512),
    )(pos, ids, total, logits, head)


def grad_kernel(pos, ids, total, total_a, total_b, logits, mine, other, adv, mine_f, other_f):
    student = total[1:2, :] - jnp.log(total[0:1, :])
    adv[:, 0:256] = (total_a[1:2, :] - jnp.log(total_a[0:1, :])) - student[:, 0:256]
    adv[:, 256:512] = (total_b[1:2, :] - jnp.log(total_b[0:1, :])) - student[:, 256:512]
    norm = jnp.log(total[0:1, :])
    for r in range(8):
        for out, core in ((mine_f, pos[17]), (other_f, 1 - pos[17])):
            start = pl.multiple_of(pos[9 + r] * 144 + core * 72, 8)
            rows = lax.broadcasted_iota(jnp.int32, (72, 512), 0) + (pos[8] + start)
            onehot = jnp.where(rows == ids[...], 1.0, 0.0)
            probs = jnp.exp(logits[pl.ds(start, 72), :] - norm)
            out[r * 72:(r + 1) * 72, :] = adv[...] * (probs - onehot)
    mine[...] = mine_f[...].astype(BF16)
    other[...] = other_f[...].astype(BF16)


def logit_grads(pos, ids, total, total_a, total_b, logits):
    v = logits.shape[0]
    half = v // 2
    return pl.pallas_call(
        grad_kernel,
        in_specs=[SMEM, whole((1, 512)), whole((8, 512)), whole((8, 256)), whole((8, 256)), whole((v, 512))],
        out_specs=[whole((half, 512)), whole((half, 512)), whole((1, 512))],
        out_shape=[jax.ShapeDtypeStruct((half, 512), BF16)] * 2 + [jax.ShapeDtypeStruct((1, 512), F32)],
        scratch_shapes=[pltpu.VMEM((half, 512), F32)] * 2,
        compiler_params=params(40),
        cost_estimate=pl.CostEstimate(flops=4 * v * 512, bytes_accessed=6 * v * 512, transcendentals=v * 512),
    )(pos, ids, total, total_a, total_b, logits)


def head_kernel(first, grad_mine, grad_from, hidden, hidden_from, *outs):
    rows = slice(first * 72, (first + len(outs)) * 72)
    product = lax.dot_general(grad_mine[rows, :], hidden[...], NN, preferred_element_type=F32)
    product += lax.dot_general(grad_from[rows, :], hidden_from[...], NN, preferred_element_type=F32)
    for i, out in enumerate(outs):
        out[...] = product[i * 72:(i + 1) * 72, :].astype(out.dtype)


def head_parts(first, types, grad_mine, grad_from, hidden, hidden_from, tile=512):
    half, d = grad_mine.shape[0], hidden.shape[1]
    n = len(types)
    column = lambda j: (0, j)
    return pl.pallas_call(
        functools.partial(head_kernel, first),
        grid=(d // tile,),
        in_specs=[whole((half, 512))] * 2 + [pl.BlockSpec((512, tile), column)] * 2,
        out_specs=[pl.BlockSpec((72, tile), column)] * n,
        out_shape=[jax.ShapeDtypeStruct((72, d), t) for t in types],
        compiler_params=params(40),
        cost_estimate=pl.CostEstimate(flops=2 * n * 72 * 1024 * d, bytes_accessed=4096 * d + n * 72 * 4 * d, transcendentals=0),
    )(grad_mine, grad_from, hidden, hidden_from)


def group_sum(a):
    around = a + send(a, X_UP) + send(a, X_DOWN) + send(a, X_FAR)
    return around + send(around, Y_HI)


def on_device(student_hidden, teacher_hidden, student_head, teacher_head, sampled_ids):
    dp, v = lax.axis_index("dp"), lax.axis_index("vocab")
    y_lo, z, core, x, y_hi = dp // 8, (dp // 2) % 4, dp % 2, v // 2, v % 2
    places = [((x + dx) % 4) * 2 + (y_hi + dy) % 2 for dx, dy in REL]
    order = ((2, 1), (-1, 1), (1, 1), (2, 0), (-1, 0), (1, 0), (0, 1), (0, 0))
    chips = [((y_lo + dy) % 2) * 4 + (z + dz) % 4 for dz, dy in order]
    pos = jnp.stack([*places, v * student_head.shape[0], *chips, core]).astype(jnp.int32)

    ids_near = send(sampled_ids, Y_HI)
    ids = jnp.where(lax.iota(jnp.int32, 512) // 64 % 2 == y_hi, sampled_ids, ids_near)
    ids = ids.reshape(8, 2, 32).transpose(1, 0, 2).reshape(1, 512)

    own = student_hidden
    left, right, near = send(own, X_UP), send(own, X_DOWN), send(own, Y_HI)
    left_near, right_near = send(near, X_UP), send(near, X_DOWN)
    far_a, far_b = send(left[:32], X_UP), send(right[32:], X_DOWN)
    far_near_a, far_near_b = send(far_a, Y_HI), send(far_b, Y_HI)
    s_blocks = (own, left, right, near, left_near, right_near, far_a, far_b, far_near_a, far_near_b)

    t_a = after(teacher_hidden[:32], left, right, near)
    l_a, r_a, n_a = send(t_a, X_UP), send(t_a, X_DOWN), send(t_a, Y_HI)
    ln_a, rn_a, f_a = send(n_a, X_UP), send(n_a, X_DOWN), send(l_a, X_UP)
    fn_a = send(f_a, Y_HI)
    t_b = after(teacher_hidden[32:], l_a, r_a, n_a)
    l_b, r_b, n_b = send(t_b, X_UP), send(t_b, X_DOWN), send(t_b, Y_HI)
    ln_b, rn_b, f_b = send(n_b, X_UP), send(n_b, X_DOWN), send(r_b, X_DOWN)
    fn_b = send(f_b, Y_HI)

    logits, hidden, stats = student_logits(pos, ids, s_blocks, student_head)
    hidden_from = send(hidden, CORE)
    total = group_sum(stats)
    g_own, g_left, g_right, g_near, g_ln, g_rn, g_fa, g_fb, g_fn = hidden_parts(pos, ids, total, logits, student_head)

    stats_a = teacher_stats(pos, ids[:, :256], (t_a, l_a, r_a, f_a, n_a, ln_a, rn_a, fn_a), teacher_head)
    total_a = group_sum(stats_a)
    stats_b = teacher_stats(pos, ids[:, 256:], (t_b, l_b, r_b, f_b, n_b, ln_b, rn_b, fn_b), teacher_head)
    total_b = group_sum(stats_b)

    from_fn = send(g_fn, Y_HI).astype(F32)
    from_fa = send((g_fa + from_fn[:32]).astype(BF16), X_DOWN).astype(F32)
    from_fb = send((g_fb + from_fn[32:]).astype(BF16), X_UP).astype(F32)
    near_sum = g_near + send(g_ln, X_DOWN).astype(F32) + send(g_rn, X_UP).astype(F32)
    left_sum = jnp.concatenate([g_left[:32] + from_fa, g_left[32:]])
    right_sum = jnp.concatenate([g_right[:32], g_right[32:] + from_fb])
    hidden_sum = (
        g_own
        + send(near_sum.astype(BF16), Y_HI).astype(F32)
        + send(left_sum.astype(BF16), X_DOWN).astype(F32)
        + send(right_sum.astype(BF16), X_UP).astype(F32)
    )

    mine, other, adv = logit_grads(pos, ids, total, total_a, total_b, logits)
    from_core = send(other, CORE)
    h_fl, h_ll, h_rl, h_f = head_parts(0, (BF16, BF16, BF16, F32), mine, from_core, hidden, hidden_from)
    h_l, h_r, h_y, h_own = head_parts(4, (F32,) * 4, mine, from_core, hidden, hidden_from)
    far = h_f + send(h_fl, Y_LO).astype(F32)
    cut = far.shape[1] // 2
    far = far.astype(BF16)
    far_left, far_right = send(far[:, :cut], Z_DOWN).astype(F32), send(far[:, cut:], Z_UP).astype(F32)
    y_sum = h_y + send(h_ll, Z_DOWN).astype(F32) + send(h_rl, Z_UP).astype(F32)
    l_sum = jnp.concatenate([h_l[:, :cut] + far_left, h_l[:, cut:]], axis=1)
    r_sum = jnp.concatenate([h_r[:, :cut], h_r[:, cut:] + far_right], axis=1)
    head_sum = (
        h_own
        + send(y_sum.astype(BF16), Y_LO).astype(F32)
        + send(l_sum.astype(BF16), Z_DOWN).astype(F32)
        + send(r_sum.astype(BF16), Z_UP).astype(F32)
    )

    own_adv = jnp.concatenate([lax.dynamic_slice(adv[0], (h * 256 + places[0] * 32,), (32,)) for h in range(2)])
    return (own_adv[:, None] * hidden_sum).astype(BF16), head_sum.astype(BF16)


def solution(mesh):
    in_specs = (
        P(("dp", "vocab"), None),
        P(("dp", "vocab"), None),
        P("vocab", None),
        P("vocab", None),
        P("dp"),
    )
    out_specs = (P(("dp", "vocab"), None), P(("vocab", "dp"), None))
    return jax.shard_map(
        on_device, mesh=mesh, in_specs=in_specs, out_specs=out_specs, check_vma=False
    )
```

```python
import functools

import jax
import jax.numpy as jnp
from jax import lax
from jax.experimental import pallas as pl
from jax.experimental.pallas import tpu as pltpu
from jax.sharding import PartitionSpec as P

BF16 = jnp.bfloat16
F32 = jnp.float32
AXES = ("dp", "vocab")

REL = ((0, 0), (-1, 0), (1, 0), (2, 0), (0, 1), (-1, 1), (1, 1), (2, 1))


def pairs(move):
    out = []
    for i in range(128):
        dp, v = i // 8, i % 8
        y_lo, z, core, x, y_hi = dp // 8, (dp // 2) % 4, dp % 2, v // 2, v % 2
        x, y, z, core = move(x, y_hi * 2 + y_lo, z, core)
        x, y, z = x % 4, y % 4, z % 4
        out.append((i, (((y % 2) * 4 + z) * 2 + core) * 8 + x * 2 + y // 2))
    return out


X_UP = pairs(lambda x, y, z, c: (x + 1, y, z, c))
X_DOWN = pairs(lambda x, y, z, c: (x - 1, y, z, c))
X_FAR = pairs(lambda x, y, z, c: (x + 2, y, z, c))
Y_HI = pairs(lambda x, y, z, c: (x, 3 - y, z, c))
Z_UP = pairs(lambda x, y, z, c: (x, y, z + 1, c))
Z_DOWN = pairs(lambda x, y, z, c: (x, y, z - 1, c))
Y_LO = pairs(lambda x, y, z, c: (x, y ^ 1, z, c))
CORE = pairs(lambda x, y, z, c: (x, y, z, 1 - c))


def send(a, to):
    return lax.ppermute(a, AXES, to)


class Link:
    def __init__(self, to, ahead=2):
        self.to, self.ahead, self.sent = to, ahead, []

    def __call__(self, a):
        if len(self.sent) >= self.ahead:
            a = after(a, self.sent[-self.ahead])
        self.sent.append(send(a, self.to))
        return self.sent[-1]


def after(a, *others):
    return lax.optimization_barrier((a, *others))[0]


def params(mib):
    return pltpu.CompilerParams(vmem_limit_bytes=mib * 2**20)


COST = pl.CostEstimate(flops=20_000_000_000, bytes_accessed=20_000_000, transcendentals=0)

VMEM = pl.BlockSpec(memory_space=pltpu.VMEM)


def kernel_call(body, arrays, outs, scratch, mib):
    return pl.pallas_call(
        body,
        in_specs=[VMEM] * len(arrays),
        out_specs=[VMEM] * len(outs),
        out_shape=[jax.ShapeDtypeStruct(shape, dtype) for shape, dtype in outs],
        scratch_shapes=[pltpu.VMEM(shape, dtype) for shape, dtype in scratch],
        compiler_params=params(mib),
        cost_estimate=COST,
    )(*arrays)


class Place:
    def __init__(self):
        dp, v = lax.axis_index("dp"), lax.axis_index("vocab")
        self.y_lo, self.z, self.core = lax.div(dp, 8), lax.rem(lax.div(dp, 2), 4), lax.rem(dp, 2)
        self.vocab, self.x, self.y_hi = v, lax.div(v, 2), lax.rem(v, 2)

    def block(self, r):
        dx, dy = REL[r]
        owner = lax.rem(self.x + (dx + 4), 4) * 2 + lax.rem(self.y_hi + dy, 2)
        return pl.multiple_of(owner * 64, 64)

    def chip(self, dz, dy):
        return lax.rem(self.y_lo + dy, 2) * 4 + lax.rem(self.z + (dz + 4), 4)

    def ids(self, own, near):
        half = lax.rem(lax.div(lax.broadcasted_iota(jnp.int32, (1, 512), 1), 64), 2)
        return jnp.where(half == self.y_hi, own[...].reshape(1, 512), near[...].reshape(1, 512))


def fold(a):
    return jnp.sum(a.reshape(a.shape[0] // 8, 8, a.shape[1]), axis=0)


NT = (((1,), (1,)), ((), ()))
NN = (((1,), (0,)), ((), ()))
TILE = 384
WIDE = 512
STATS = (8, 512)


def put_blocks(place, blocks, hidden):
    for r, block in enumerate(blocks):
        hidden[pl.ds(place.block(r), 64), :] = block[...]


def put_stats(stats, sums, picks):
    stats[...] = jnp.zeros_like(stats)
    stats[0:1, :] = jnp.sum(sums, axis=0, keepdims=True)
    stats[1:2, :] = jnp.sum(picks, axis=0, keepdims=True)


def student_kernel(ids_own, ids_near, head, *refs):
    blocks, (logits, hidden, stats) = refs[:8], refs[8:]
    place = Place()
    put_blocks(place, blocks, hidden)
    ids = place.ids(ids_own, ids_near)
    sums = picks = 0.0
    for j in range(head.shape[0] // TILE):
        tile = slice(j * TILE, (j + 1) * TILE)
        out = lax.dot_general(head[tile, :], hidden[...], NT, preferred_element_type=F32)
        logits[tile, :] = out
        rows = lax.broadcasted_iota(jnp.int32, out.shape, 0) + (place.vocab * head.shape[0] + j * TILE)
        sums += fold(jnp.exp(out))
        picks += fold(jnp.where(rows == ids, out, 0.0))
    put_stats(stats, sums, picks)


def student_logits(ids, blocks, head):
    v, d = head.shape
    outs = [((v, 512), F32), ((512, d), BF16), (STATS, F32)]
    return kernel_call(student_kernel, (*ids, head, *blocks), outs, [], 6)


def teacher_first_kernel(head, *refs):
    blocks, (logits, hidden) = refs[:8], refs[8:]
    put_blocks(Place(), blocks, hidden)
    for j in range(head.shape[0] // TILE):
        tile = slice(j * TILE, (j + 1) * TILE)
        logits[tile, :] = lax.dot_general(
            head[tile, 0:hidden.shape[1]], hidden[...], NT, preferred_element_type=F32
        )


def teacher_first(blocks, head):
    v, d = head.shape
    return kernel_call(teacher_first_kernel, (head, *blocks), [((v, 512), F32)], [((512, d // 2), BF16)], 8)[0]


def teacher_second_kernel(ids_own, ids_near, head, logits, *refs):
    blocks, (stats, hidden) = refs[:8], refs[8:]
    place = Place()
    put_blocks(place, blocks, hidden)
    ids = place.ids(ids_own, ids_near)
    sums = picks = 0.0
    for j in range(head.shape[0] // TILE):
        tile = slice(j * TILE, (j + 1) * TILE)
        out = logits[tile, :] + lax.dot_general(
            head[tile, hidden.shape[1]:], hidden[...], NT, preferred_element_type=F32
        )
        rows = lax.broadcasted_iota(jnp.int32, out.shape, 0) + (place.vocab * head.shape[0] + j * TILE)
        sums += fold(jnp.exp(out))
        picks += fold(jnp.where(rows == ids, out, 0.0))
    put_stats(stats, sums, picks)


def teacher_second(ids, blocks, head, logits):
    scratch = [((512, head.shape[1] // 2), BF16)]
    return kernel_call(teacher_second_kernel, (*ids, head, logits, *blocks), [(STATS, F32)], scratch, 8)[0]


def hidden_kernel(ids_own, ids_near, total, logits, head, own, near, far, far_near, lefts, rights, grad_t, product):
    place = Place()
    ids = place.ids(ids_own, ids_near)
    norm = jnp.log(total[0:1, :])
    for k in range(head.shape[0] // 128):
        part = slice(k * 128, (k + 1) * 128)
        rows = lax.broadcasted_iota(jnp.int32, (128, 512), 0) + (place.vocab * head.shape[0] + k * 128)
        onehot = jnp.where(rows == ids, 1.0, 0.0)
        grad_t[:, part] = (jnp.exp(logits[part, :] - norm) - onehot).T.astype(BF16)

    outs = ((own, 0), (lefts, 0), (rights, 0), (far, 0), (near, 0), (lefts, 64), (rights, 64), (far_near, 0))
    for j in range(head.shape[1] // WIDE):
        tile = slice(j * WIDE, (j + 1) * WIDE)
        product[...] = lax.dot_general(grad_t[...], head[:, tile], NN, preferred_element_type=F32)
        for r, (out, row) in enumerate(outs):
            out[row:row + 64, tile] = product[pl.ds(place.block(r), 64), :].astype(out.dtype)


def hidden_parts(ids, total, logits, head):
    v, d = head.shape
    outs = [((64, d), F32)] * 3 + [((64, d), BF16)] + [((128, d), BF16)] * 2
    scratch = [((512, v), BF16), ((512, WIDE), F32)]
    return kernel_call(hidden_kernel, (*ids, total, logits, head), outs, scratch, 6)


CHIPS = ((2, 1), (-1, 1), (1, 1), (2, 0), (-1, 0), (1, 0), (0, 1), (0, 0))


def grad_kernel(ids_own, ids_near, total, teacher, logits, mine, other, adv, mine_f, other_f):
    place = Place()
    ids = place.ids(ids_own, ids_near)
    norm = jnp.log(total[0:1, :])
    adv[...] = (teacher[1:2, :] - jnp.log(teacher[0:1, :])) - (total[1:2, :] - norm)
    for r, chip in enumerate(CHIPS):
        for out, core in ((mine_f, place.core), (other_f, 1 - place.core)):
            start = pl.multiple_of(place.chip(*chip) * 144 + core * 72, 8)
            rows = lax.broadcasted_iota(jnp.int32, (72, 512), 0) + (place.vocab * logits.shape[0] + start)
            onehot = jnp.where(rows == ids, 1.0, 0.0)
            probs = jnp.exp(logits[pl.ds(start, 72), :] - norm)
            out[r * 72:(r + 1) * 72, :] = adv[...] * (probs - onehot)
    mine[...] = mine_f[...].astype(BF16)
    other[...] = other_f[...].astype(BF16)


def logit_grads(ids, total, teacher, logits):
    half = logits.shape[0] // 2
    outs = [((half, 512), BF16)] * 2 + [((1, 512), F32)]
    return kernel_call(grad_kernel, (*ids, total, teacher, logits), outs, [((half, 512), F32)] * 2, 5)


def head_kernel(first, grad_mine, grad_from, hidden, hidden_from, *outs):
    rows = slice(first * 72, (first + len(outs)) * 72)
    for j in range(hidden.shape[1] // WIDE):
        tile = slice(j * WIDE, (j + 1) * WIDE)
        product = lax.dot_general(grad_mine[rows, :], hidden[:, tile], NN, preferred_element_type=F32)
        product += lax.dot_general(grad_from[rows, :], hidden_from[:, tile], NN, preferred_element_type=F32)
        for i, out in enumerate(outs):
            out[:, tile] = product[i * 72:(i + 1) * 72, :].astype(out.dtype)


def head_parts(first, types, grad_mine, grad_from, hidden, hidden_from):
    outs = [((72, hidden.shape[1]), t) for t in types]
    return kernel_call(functools.partial(head_kernel, first), (grad_mine, grad_from, hidden, hidden_from), outs, [], 4)


def finish_kernel(adv, own, lefts, rights, far, near, out):
    place = Place()
    total = own[...] + lefts[0:64, :].astype(F32) + rights[0:64, :].astype(F32)
    total += far[...].astype(F32) + near[...].astype(F32)
    token = lax.broadcasted_iota(jnp.int32, (64, 512), 0) + place.block(0)
    at = lax.broadcasted_iota(jnp.int32, (64, 512), 1)
    mine = jnp.sum(jnp.where(token == at, adv[...], 0.0), axis=1, keepdims=True)
    out[...] = (mine * total).astype(out.dtype)


def group_sum(a):
    around = a + send(a, X_UP) + send(a, X_DOWN) + send(a, X_FAR)
    return around + send(around, Y_HI)


def on_device(student_hidden, teacher_hidden, student_head, teacher_head, sampled_ids):
    ids = (sampled_ids, send(sampled_ids, Y_HI))

    up, down, over = Link(X_UP), Link(X_DOWN), Link(Y_HI)
    half = teacher_hidden.shape[1] // 2
    t_a, t_b = teacher_hidden[:, :half], teacher_hidden[:, half:]
    left, right, near = up(student_hidden), down(student_hidden), over(student_hidden)
    l_a, r_a, near_a = up(t_a), down(t_a), over(t_a)
    far, right_near, near_b = up(left), down(near), over(t_b)
    left_near, f_a, far_near = up(near), down(r_a), over(far)
    l_b, r_b, fn_a = up(t_b), down(t_b), over(f_a)
    ln_a, rn_a = up(near_a), down(near_a)
    f_b = up(l_b)
    fn_b = over(f_b)
    ln_b, rn_b = up(near_b), down(near_b)

    blocks = (student_hidden, left, right, far, near, left_near, right_near, far_near)
    logits, hidden, stats = student_logits((ids[0], after(ids[1], l_b, r_b, near_b)), blocks, student_head)
    hidden_from = send(hidden, CORE)
    total = after(group_sum(stats), ln_a, rn_a, f_b)
    parts = hidden_parts(ids, total, logits, student_head)
    teacher_logits = teacher_first((t_a, l_a, r_a, f_a, near_a, ln_a, rn_a, fn_a), teacher_head)
    teacher_logits = after(teacher_logits, parts[0])
    stats = teacher_second(ids, (t_b, l_b, r_b, f_b, near_b, ln_b, rn_b, fn_b), teacher_head, teacher_logits)
    teacher = group_sum(stats)

    g_own, g_near, g_far, g_far_near, g_lefts, g_rights = lax.optimization_barrier((*parts, stats))[:6]
    from_lefts, from_rights, from_fn = down(g_lefts), up(g_rights), over(g_far_near)
    from_far = send((g_far + from_fn.astype(F32)).astype(BF16), X_FAR)
    g_near = g_near + from_lefts[64:].astype(F32) + from_rights[64:].astype(F32)
    from_near = over(g_near.astype(BF16))

    mine, other, adv = logit_grads(ids, total, teacher, logits)
    from_core = send(other, CORE)
    h_fl, h_ll, h_rl, h_f = head_parts(0, (BF16, BF16, BF16, F32), mine, from_core, hidden, hidden_from)
    h_l, h_r, h_y, h_own = head_parts(4, (F32,) * 4, mine, from_core, hidden, hidden_from)
    far = h_f + send(h_fl, Y_LO).astype(F32)
    cut = far.shape[1] // 2
    far = far.astype(BF16)
    far_left, far_right = send(far[:, :cut], Z_DOWN).astype(F32), send(far[:, cut:], Z_UP).astype(F32)
    y_sum = h_y + send(h_ll, Z_DOWN).astype(F32) + send(h_rl, Z_UP).astype(F32)
    l_sum = jnp.concatenate([h_l[:, :cut] + far_left, h_l[:, cut:]], axis=1)
    r_sum = jnp.concatenate([h_r[:, :cut], h_r[:, cut:] + far_right], axis=1)
    head_sum = (
        h_own
        + send(y_sum.astype(BF16), Y_LO).astype(F32)
        + send(l_sum.astype(BF16), Z_DOWN).astype(F32)
        + send(r_sum.astype(BF16), Z_UP).astype(F32)
    )
    pieces = (adv, g_own, from_lefts, from_rights, from_far, from_near)
    return kernel_call(finish_kernel, pieces, [(student_hidden.shape, BF16)], [], 4)[0], head_sum.astype(BF16)


def solution(mesh):
    in_specs = (
        P(("dp", "vocab"), None),
        P(("dp", "vocab"), None),
        P("vocab", None),
        P("vocab", None),
        P("dp"),
    )
    out_specs = (P(("dp", "vocab"), None), P(("vocab", "dp"), None))
    return jax.shard_map(
        on_device, mesh=mesh, in_specs=in_specs, out_specs=out_specs, check_vma=False
    )
```

```python
import functools

import jax
import jax.numpy as jnp
from jax import lax
from jax.experimental import pallas as pl
from jax.experimental.pallas import tpu as pltpu
from jax.sharding import PartitionSpec as P

BF16 = jnp.bfloat16
F32 = jnp.float32
AXES = ("dp", "vocab")

REL = ((0, 0), (-1, 0), (1, 0), (2, 0), (0, 1), (-1, 1), (1, 1), (2, 1))


def pairs(move):
    out = []
    for i in range(128):
        dp, v = i // 8, i % 8
        y_lo, z, core, x, y_hi = dp // 8, (dp // 2) % 4, dp % 2, v // 2, v % 2
        x, y, z, core = move(x, y_hi * 2 + y_lo, z, core)
        x, y, z = x % 4, y % 4, z % 4
        out.append((i, (((y % 2) * 4 + z) * 2 + core) * 8 + x * 2 + y // 2))
    return out


X_UP = pairs(lambda x, y, z, c: (x + 1, y, z, c))
X_DOWN = pairs(lambda x, y, z, c: (x - 1, y, z, c))
X_FAR = pairs(lambda x, y, z, c: (x + 2, y, z, c))
Y_HI = pairs(lambda x, y, z, c: (x, 3 - y, z, c))
Z_UP = pairs(lambda x, y, z, c: (x, y, z + 1, c))
Z_DOWN = pairs(lambda x, y, z, c: (x, y, z - 1, c))
Z_FAR = pairs(lambda x, y, z, c: (x, y, z + 2, c))
Y_LO = pairs(lambda x, y, z, c: (x, y ^ 1, z, c))
CORE = pairs(lambda x, y, z, c: (x, y, z, 1 - c))


def send(a, to):
    return lax.ppermute(a, AXES, to)


class Link:
    def __init__(self, to, ahead=2):
        self.to, self.ahead, self.sent = to, ahead, []

    def __call__(self, a):
        if len(self.sent) >= self.ahead:
            a = after(a, self.sent[-self.ahead])
        self.sent.append(send(a, self.to))
        return self.sent[-1]


def after(a, *others):
    return lax.optimization_barrier((a, *others))[0]


def params(mib):
    return pltpu.CompilerParams(vmem_limit_bytes=mib * 2**20)


LONG, SHORT = 20, 1


VMEM = pl.BlockSpec(memory_space=pltpu.VMEM)


def kernel_call(body, arrays, outs, scratch, mib, said=SHORT):
    return pl.pallas_call(
        body,
        in_specs=[VMEM] * len(arrays),
        out_specs=[VMEM] * len(outs),
        out_shape=[jax.ShapeDtypeStruct(shape, dtype) for shape, dtype in outs],
        scratch_shapes=[pltpu.VMEM(shape, dtype) for shape, dtype in scratch],
        compiler_params=params(mib),
        cost_estimate=pl.CostEstimate(flops=said * 10**9, bytes_accessed=said * 10**6, transcendentals=0),
    )(*arrays)


class Place:
    def __init__(self):
        dp, v = lax.axis_index("dp"), lax.axis_index("vocab")
        self.y_lo, self.z, self.core = lax.div(dp, 8), lax.rem(lax.div(dp, 2), 4), lax.rem(dp, 2)
        self.vocab, self.x, self.y_hi = v, lax.div(v, 2), lax.rem(v, 2)

    def block(self, r):
        dx, dy = REL[r]
        owner = lax.rem(self.x + (dx + 4), 4) * 2 + lax.rem(self.y_hi + dy, 2)
        return pl.multiple_of(owner * 64, 64)

    def chip(self, dz, dy):
        return lax.rem(self.y_lo + dy, 2) * 4 + lax.rem(self.z + (dz + 4), 4)


def ids_kernel(own, near, ids):
    half = lax.rem(lax.div(lax.broadcasted_iota(jnp.int32, (1, 512), 1), 64), 2)
    ids[...] = jnp.where(half == Place().y_hi, own[...].reshape(1, 512), near[...].reshape(1, 512))


def fold(a):
    return jnp.sum(a.reshape(a.shape[0] // 8, 8, a.shape[1]), axis=0)


NT = (((1,), (1,)), ((), ()))
NN = (((1,), (0,)), ((), ()))
TILE = 384
WIDE = 512
STATS = (8, 512)


def put_blocks(place, blocks, hidden):
    for r, block in enumerate(blocks):
        hidden[pl.ds(place.block(r), 64), :] = block[...]


def put_stats(stats, first, sums, picks):
    stats[first:first + 1, :] = jnp.sum(sums, axis=0, keepdims=True)
    stats[first + 1:first + 2, :] = jnp.sum(picks, axis=0, keepdims=True)


def advantage(total):
    norm = jnp.log(total[0:1, :])
    return (total[3:4, :] - jnp.log(total[2:3, :])) - (total[1:2, :] - norm), norm


def student_kernel(ids, head, *refs):
    blocks, (logits, hidden, stats) = refs[:8], refs[8:]
    place = Place()
    put_blocks(place, blocks, hidden)
    sums = picks = 0.0
    for j in range(head.shape[0] // TILE):
        tile = slice(j * TILE, (j + 1) * TILE)
        out = lax.dot_general(head[tile, :], hidden[...], NT, preferred_element_type=F32)
        logits[tile, :] = out
        rows = lax.broadcasted_iota(jnp.int32, out.shape, 0) + (place.vocab * head.shape[0] + j * TILE)
        sums += fold(jnp.exp(out))
        picks += fold(jnp.where(rows == ids[...], out, 0.0))
    stats[...] = jnp.zeros_like(stats)
    put_stats(stats, 0, sums, picks)


def student_logits(ids, blocks, head):
    v, d = head.shape
    outs = [((v, 512), F32), ((512, d), BF16), (STATS, F32)]
    return kernel_call(student_kernel, (ids, head, *blocks), outs, [], 6, LONG)


def teacher_first_kernel(head, *refs):
    blocks, (logits, hidden) = refs[:8], refs[8:]
    put_blocks(Place(), blocks, hidden)
    for j in range(head.shape[0] // TILE):
        tile = slice(j * TILE, (j + 1) * TILE)
        logits[tile, :] = lax.dot_general(
            head[tile, 0:hidden.shape[1]], hidden[...], NT, preferred_element_type=F32
        )


def teacher_first(blocks, head):
    v, d = head.shape
    return kernel_call(teacher_first_kernel, (head, *blocks), [((v, 512), F32)], [((512, d // 2), BF16)], 8, LONG)[0]


def teacher_second_kernel(ids, student_stats, head, logits, *refs):
    blocks, (stats, hidden) = refs[:8], refs[8:]
    place = Place()
    put_blocks(place, blocks, hidden)
    sums = picks = 0.0
    for j in range(head.shape[0] // TILE):
        tile = slice(j * TILE, (j + 1) * TILE)
        out = logits[tile, :] + lax.dot_general(
            head[tile, hidden.shape[1]:], hidden[...], NT, preferred_element_type=F32
        )
        rows = lax.broadcasted_iota(jnp.int32, out.shape, 0) + (place.vocab * head.shape[0] + j * TILE)
        sums += fold(jnp.exp(out))
        picks += fold(jnp.where(rows == ids[...], out, 0.0))
    stats[...] = student_stats[...]
    put_stats(stats, 2, sums, picks)


def teacher_second(ids, student_stats, blocks, head, logits):
    scratch = [((512, head.shape[1] // 2), BF16)]
    return kernel_call(teacher_second_kernel, (ids, student_stats, head, logits, *blocks), [(STATS, F32)], scratch, 8, LONG)[0]


def hidden_kernel(ids, total, logits, head, own, near, far, far_near, lefts, rights, grad_t, product):
    place = Place()
    adv, norm = advantage(total)
    for k in range(head.shape[0] // 128):
        part = slice(k * 128, (k + 1) * 128)
        rows = lax.broadcasted_iota(jnp.int32, (128, 512), 0) + (place.vocab * head.shape[0] + k * 128)
        onehot = jnp.where(rows == ids[...], 1.0, 0.0)
        grad_t[:, part] = (adv * (jnp.exp(logits[part, :] - norm) - onehot)).T.astype(BF16)

    outs = ((own, 0), (lefts, 0), (rights, 0), (far, 0), (near, 0), (lefts, 64), (rights, 64), (far_near, 0))
    for j in range(head.shape[1] // WIDE):
        tile = slice(j * WIDE, (j + 1) * WIDE)
        product[...] = lax.dot_general(grad_t[...], head[:, tile], NN, preferred_element_type=F32)
        for r, (out, row) in enumerate(outs):
            out[row:row + 64, tile] = product[pl.ds(place.block(r), 64), :].astype(out.dtype)


def hidden_parts(ids, total, logits, head):
    v, d = head.shape
    outs = [((64, d), F32)] * 3 + [((64, d), BF16)] + [((128, d), BF16)] * 2
    scratch = [((512, v), BF16), ((512, WIDE), F32)]
    return kernel_call(hidden_kernel, (ids, total, logits, head), outs, scratch, 6, LONG)


CHIPS = ((-1, 0), (-1, 1), (1, 0), (1, 1), (2, 1), (2, 0), (0, 1), (0, 0))


def grad_kernel(ids, total, logits, mine, other, mine_f, other_f):
    place = Place()
    adv, norm = advantage(total)
    for r, chip in enumerate(CHIPS):
        for out, core in ((mine_f, place.core), (other_f, 1 - place.core)):
            start = pl.multiple_of(place.chip(*chip) * 144 + core * 72, 8)
            rows = lax.broadcasted_iota(jnp.int32, (72, 512), 0) + (place.vocab * logits.shape[0] + start)
            onehot = jnp.where(rows == ids[...], 1.0, 0.0)
            probs = jnp.exp(logits[pl.ds(start, 72), :] - norm)
            out[r * 72:(r + 1) * 72, :] = adv * (probs - onehot)
    mine[...] = mine_f[...].astype(BF16)
    other[...] = other_f[...].astype(BF16)


def logit_grads(ids, total, logits):
    half = logits.shape[0] // 2
    outs = [((half, 512), BF16)] * 2
    return kernel_call(grad_kernel, (ids, total, logits), outs, [((half, 512), F32)] * 2, 5, LONG)


def head_kernel(first, grad_mine, grad_from, hidden, hidden_from, *outs):
    n = sum(out.shape[0] for out in outs)
    rows = slice(first, first + n)
    for j in range(hidden.shape[1] // WIDE):
        tile = slice(j * WIDE, (j + 1) * WIDE)
        product = lax.dot_general(grad_mine[rows, :], hidden[:, tile], NN, preferred_element_type=F32)
        product += lax.dot_general(grad_from[rows, :], hidden_from[:, tile], NN, preferred_element_type=F32)
        start = 0
        for out in outs:
            out[:, tile] = product[start:start + out.shape[0], :].astype(out.dtype)
            start += out.shape[0]


def head_parts(first, outs, said, grad_mine, grad_from, hidden, hidden_from):
    outs = [((n, hidden.shape[1]), t) for n, t in outs]
    arrays = (grad_mine, grad_from, hidden, hidden_from)
    return kernel_call(functools.partial(head_kernel, first), arrays, outs, [], 4, said)


def finish_kernel(own, lefts, rights, far, near, out):
    total = own[...] + lefts[0:64, :].astype(F32) + rights[0:64, :].astype(F32)
    out[...] = (total + far[...].astype(F32) + near[...].astype(F32)).astype(out.dtype)


def group_sum(a):
    around = a + send(a, X_UP) + send(a, X_DOWN) + send(a, X_FAR)
    return around + send(around, Y_HI)


def on_device(student_hidden, teacher_hidden, student_head, teacher_head, sampled_ids):
    up, down, over = Link(X_UP), Link(X_DOWN), Link(Y_HI)
    half = teacher_hidden.shape[1] // 2
    t_a, t_b = teacher_hidden[:, :half], teacher_hidden[:, half:]
    left, right, near = up(student_hidden), down(student_hidden), over(student_hidden)
    ids_near = send(sampled_ids, Y_HI)
    l_a, r_a, near_a = up(t_a), down(t_a), over(after(t_a, ids_near))
    near_b = over(t_b)
    ids = kernel_call(ids_kernel, (sampled_ids, ids_near), [((1, 512), jnp.int32)], [], 1, LONG)[0]
    t_b = after(t_b, ids)
    far, right_near = up(left), down(near)
    left_near, f_a, far_near = up(near), down(r_a), over(far)
    l_b, r_b = up(t_b), down(t_b)
    ln_a, rn_a, fn_a = up(near_a), down(near_a), over(f_a)
    f_b = up(l_b)
    fn_b = over(f_b)
    ln_b, rn_b = up(near_b), down(near_b)

    blocks = (student_hidden, left, right, far, near, left_near, right_near, far_near)
    logits, hidden, student_stats = student_logits(ids, blocks, student_head)
    hidden_from = send(hidden, CORE)
    teacher_logits = teacher_first((t_a, l_a, r_a, f_a, near_a, ln_a, rn_a, fn_a), teacher_head)
    blocks = (t_b, l_b, r_b, f_b, near_b, ln_b, rn_b, fn_b)
    total = group_sum(teacher_second(ids, student_stats, blocks, teacher_head, teacher_logits))

    mine, other = logit_grads(ids, total, logits)
    grads = (mine, send(other, CORE), hidden, hidden_from)
    h_lefts, h_rights = head_parts(0, ((144, BF16), (144, BF16)), SHORT, *grads)
    grads = (after(mine, h_lefts), *grads[1:])
    h_fl, h_f, h_y, h_own = head_parts(288, ((72, BF16), (72, F32), (72, F32), (72, F32)), LONG, *grads)
    from_lefts, from_rights, from_fl = send(h_lefts, Z_DOWN), send(h_rights, Z_UP), send(h_fl, Y_LO)
    from_f = send(after((h_f + from_fl.astype(F32)).astype(BF16), from_lefts), Z_FAR)
    h_y = h_y + from_lefts[72:].astype(F32) + from_rights[72:].astype(F32)
    from_y = send(h_y.astype(BF16), Y_LO)
    head_sum = h_own + from_lefts[:72].astype(F32) + from_rights[:72].astype(F32)
    head_sum = head_sum + from_f.astype(F32) + from_y.astype(F32)

    g_own, g_near, g_far, g_far_near, g_lefts, g_rights = hidden_parts(ids, after(total, h_fl), logits, student_head)
    from_lefts, from_rights, from_fn = send(g_lefts, X_DOWN), send(g_rights, X_UP), send(after(g_far_near, from_fl), Y_HI)
    from_far = send((g_far + from_fn.astype(F32)).astype(BF16), X_FAR)
    g_near = g_near + from_lefts[64:].astype(F32) + from_rights[64:].astype(F32)
    from_near = send(g_near.astype(BF16), Y_HI)
    pieces = (g_own, from_lefts, from_rights, from_far, from_near)
    return kernel_call(finish_kernel, pieces, [(student_hidden.shape, BF16)], [], 4)[0], head_sum.astype(BF16)


def solution(mesh):
    in_specs = (
        P(("dp", "vocab"), None),
        P(("dp", "vocab"), None),
        P("vocab", None),
        P("vocab", None),
        P("dp"),
    )
    out_specs = (P(("dp", "vocab"), None), P(("vocab", "dp"), None))
    return jax.shard_map(
        on_device, mesh=mesh, in_specs=in_specs, out_specs=out_specs, check_vma=False
    )
```

```python
import functools

import jax
import jax.numpy as jnp
from jax import lax
from jax.experimental import pallas as pl
from jax.experimental.pallas import tpu as pltpu
from jax.sharding import PartitionSpec as P

BF16 = jnp.bfloat16
F32 = jnp.float32
AXES = ("dp", "vocab")

REL = ((0, 0), (-1, 0), (1, 0), (2, 0), (0, 1), (-1, 1), (1, 1), (2, 1))


def pairs(move):
    out = []
    for i in range(128):
        dp, v = i // 8, i % 8
        y_lo, z, core, x, y_hi = dp // 8, (dp // 2) % 4, dp % 2, v // 2, v % 2
        x, y, z, core = move(x, y_hi * 2 + y_lo, z, core)
        x, y, z = x % 4, y % 4, z % 4
        out.append((i, (((y % 2) * 4 + z) * 2 + core) * 8 + x * 2 + y // 2))
    return out


X_UP = pairs(lambda x, y, z, c: (x + 1, y, z, c))
X_DOWN = pairs(lambda x, y, z, c: (x - 1, y, z, c))
X_FAR = pairs(lambda x, y, z, c: (x + 2, y, z, c))
Y_HI = pairs(lambda x, y, z, c: (x, 3 - y, z, c))
Z_UP = pairs(lambda x, y, z, c: (x, y, z + 1, c))
Z_DOWN = pairs(lambda x, y, z, c: (x, y, z - 1, c))
Z_FAR = pairs(lambda x, y, z, c: (x, y, z + 2, c))
Y_LO = pairs(lambda x, y, z, c: (x, y ^ 1, z, c))
CORE = pairs(lambda x, y, z, c: (x, y, z, 1 - c))


def send(a, to):
    return lax.ppermute(a, AXES, to)


class Link:
    def __init__(self, to, ahead=2):
        self.to, self.ahead, self.sent = to, ahead, []

    def __call__(self, a):
        if len(self.sent) >= self.ahead:
            a = after(a, self.sent[-self.ahead])
        self.sent.append(send(a, self.to))
        return self.sent[-1]


def after(a, *others):
    return lax.optimization_barrier((a, *others))[0]


def params(mib):
    return pltpu.CompilerParams(vmem_limit_bytes=mib * 2**20)


LONG, SHORT = 20, 1


VMEM = pl.BlockSpec(memory_space=pltpu.VMEM)


def kernel_call(body, arrays, outs, scratch, mib, said=SHORT):
    return pl.pallas_call(
        body,
        in_specs=[VMEM] * len(arrays),
        out_specs=[VMEM] * len(outs),
        out_shape=[jax.ShapeDtypeStruct(shape, dtype) for shape, dtype in outs],
        scratch_shapes=[pltpu.VMEM(shape, dtype) for shape, dtype in scratch],
        compiler_params=params(mib),
        cost_estimate=pl.CostEstimate(flops=said * 10**9, bytes_accessed=said * 10**6, transcendentals=0),
    )(*arrays)


class Place:
    def __init__(self):
        dp, v = lax.axis_index("dp"), lax.axis_index("vocab")
        self.y_lo, self.z, self.core = lax.div(dp, 8), lax.rem(lax.div(dp, 2), 4), lax.rem(dp, 2)
        self.vocab, self.x, self.y_hi = v, lax.div(v, 2), lax.rem(v, 2)

    def block(self, r):
        dx, dy = REL[r]
        owner = lax.rem(self.x + (dx + 4), 4) * 2 + lax.rem(self.y_hi + dy, 2)
        return pl.multiple_of(owner * 64, 64)

    def chip(self, dz, dy):
        return lax.rem(self.y_lo + dy, 2) * 4 + lax.rem(self.z + (dz + 4), 4)


def ids_kernel(own, near, ids):
    half = lax.rem(lax.div(lax.broadcasted_iota(jnp.int32, (1, 512), 1), 64), 2)
    ids[...] = jnp.where(half == Place().y_hi, own[...].reshape(1, 512), near[...].reshape(1, 512))


def fold(a):
    return jnp.sum(a.reshape(a.shape[0] // 8, 8, a.shape[1]), axis=0)


NT = (((1,), (1,)), ((), ()))
NN = (((1,), (0,)), ((), ()))
TILE = 384
WIDE = 512
STATS = (8, 512)


def put_blocks(place, blocks, hidden):
    for r, block in enumerate(blocks):
        hidden[pl.ds(place.block(r), 64), :] = block[...]


def put_stats(stats, first, sums, picks):
    stats[first:first + 1, :] = jnp.sum(sums, axis=0, keepdims=True)
    stats[first + 1:first + 2, :] = jnp.sum(picks, axis=0, keepdims=True)


def advantage(total):
    norm = jnp.log(total[0:1, :])
    return (total[3:4, :] - jnp.log(total[2:3, :])) - (total[1:2, :] - norm), norm


def student_kernel(ids, head, *refs):
    blocks, (logits, hidden, stats) = refs[:8], refs[8:]
    place = Place()
    put_blocks(place, blocks, hidden)
    sums = picks = 0.0
    for j in range(head.shape[0] // TILE):
        tile = slice(j * TILE, (j + 1) * TILE)
        out = lax.dot_general(head[tile, :], hidden[...], NT, preferred_element_type=F32)
        logits[tile, :] = out
        rows = lax.broadcasted_iota(jnp.int32, out.shape, 0) + (place.vocab * head.shape[0] + j * TILE)
        sums += fold(jnp.exp(out))
        picks += fold(jnp.where(rows == ids[...], out, 0.0))
    stats[...] = jnp.zeros_like(stats)
    put_stats(stats, 0, sums, picks)


def student_logits(ids, blocks, head):
    v, d = head.shape
    outs = [((v, 512), F32), ((512, d), BF16), (STATS, F32)]
    return kernel_call(student_kernel, (ids, head, *blocks), outs, [], 6, LONG)


def teacher_first_kernel(head, *refs):
    blocks, (logits, hidden) = refs[:8], refs[8:]
    put_blocks(Place(), blocks, hidden)
    for j in range(head.shape[0] // TILE):
        tile = slice(j * TILE, (j + 1) * TILE)
        logits[tile, :] = lax.dot_general(
            head[tile, 0:hidden.shape[1]], hidden[...], NT, preferred_element_type=F32
        )


def teacher_first(blocks, head):
    v, d = head.shape
    return kernel_call(teacher_first_kernel, (head, *blocks), [((v, 512), F32)], [((512, d // 2), BF16)], 8, LONG)[0]


def teacher_second_kernel(ids, student_stats, head, logits, *refs):
    blocks, (stats, hidden) = refs[:8], refs[8:]
    place = Place()
    put_blocks(place, blocks, hidden)
    sums = picks = 0.0
    for j in range(head.shape[0] // TILE):
        tile = slice(j * TILE, (j + 1) * TILE)
        out = logits[tile, :] + lax.dot_general(
            head[tile, hidden.shape[1]:], hidden[...], NT, preferred_element_type=F32
        )
        rows = lax.broadcasted_iota(jnp.int32, out.shape, 0) + (place.vocab * head.shape[0] + j * TILE)
        sums += fold(jnp.exp(out))
        picks += fold(jnp.where(rows == ids[...], out, 0.0))
    stats[...] = student_stats[...]
    put_stats(stats, 2, sums, picks)


def teacher_second(ids, student_stats, blocks, head, logits):
    scratch = [((512, head.shape[1] // 2), BF16)]
    return kernel_call(teacher_second_kernel, (ids, student_stats, head, logits, *blocks), [(STATS, F32)], scratch, 8, LONG)[0]


def hidden_kernel(ids, total, logits, head, own, near, far, far_near, lefts, rights, grad_t, product):
    place = Place()
    adv, norm = advantage(total)
    for k in range(head.shape[0] // 128):
        part = slice(k * 128, (k + 1) * 128)
        rows = lax.broadcasted_iota(jnp.int32, (128, 512), 0) + (place.vocab * head.shape[0] + k * 128)
        onehot = jnp.where(rows == ids[...], 1.0, 0.0)
        grad_t[:, part] = (adv * (jnp.exp(logits[part, :] - norm) - onehot)).T.astype(BF16)

    outs = ((own, 0), (lefts, 0), (rights, 0), (far, 0), (near, 0), (lefts, 64), (rights, 64), (far_near, 0))
    for j in range(head.shape[1] // WIDE):
        tile = slice(j * WIDE, (j + 1) * WIDE)
        product[...] = lax.dot_general(grad_t[...], head[:, tile], NN, preferred_element_type=F32)
        for r, (out, row) in enumerate(outs):
            out[row:row + 64, tile] = product[pl.ds(place.block(r), 64), :].astype(out.dtype)


def hidden_parts(ids, total, logits, head):
    v, d = head.shape
    outs = [((64, d), F32)] * 3 + [((64, d), BF16)] + [((128, d), BF16)] * 2
    scratch = [((512, v), BF16), ((512, WIDE), F32)]
    return kernel_call(hidden_kernel, (ids, total, logits, head), outs, scratch, 6, LONG)


CHIPS = ((-1, 0), (-1, 1), (1, 0), (1, 1), (2, 1), (2, 0), (0, 1), (0, 0))


def grad_kernel(ids, total, logits, mine, other, mine_f, other_f):
    place = Place()
    adv, norm = advantage(total)
    for r, chip in enumerate(CHIPS):
        for out, core in ((mine_f, place.core), (other_f, 1 - place.core)):
            start = pl.multiple_of(place.chip(*chip) * 144 + core * 72, 8)
            rows = lax.broadcasted_iota(jnp.int32, (72, 512), 0) + (place.vocab * logits.shape[0] + start)
            onehot = jnp.where(rows == ids[...], 1.0, 0.0)
            probs = jnp.exp(logits[pl.ds(start, 72), :] - norm)
            out[r * 72:(r + 1) * 72, :] = adv * (probs - onehot)
    mine[...] = mine_f[...].astype(BF16)
    other[...] = other_f[...].astype(BF16)


def logit_grads(ids, total, logits):
    half = logits.shape[0] // 2
    outs = [((half, 512), BF16)] * 2
    return kernel_call(grad_kernel, (ids, total, logits), outs, [((half, 512), F32)] * 2, 5, LONG)


def head_kernel(first, grad_mine, grad_from, hidden, hidden_from, *outs):
    n = sum(out.shape[0] for out in outs)
    rows = slice(first, first + n)
    for j in range(hidden.shape[1] // WIDE):
        tile = slice(j * WIDE, (j + 1) * WIDE)
        product = lax.dot_general(grad_mine[rows, :], hidden[:, tile], NN, preferred_element_type=F32)
        product += lax.dot_general(grad_from[rows, :], hidden_from[:, tile], NN, preferred_element_type=F32)
        start = 0
        for out in outs:
            out[:, tile] = product[start:start + out.shape[0], :].astype(out.dtype)
            start += out.shape[0]


def head_parts(first, outs, said, grad_mine, grad_from, hidden, hidden_from):
    outs = [((n, hidden.shape[1]), t) for n, t in outs]
    arrays = (grad_mine, grad_from, hidden, hidden_from)
    return kernel_call(functools.partial(head_kernel, first), arrays, outs, [], 4, said)


def pass_on_kernel(near, far, lefts, rights, far_near, near_out, far_out):
    n = near.shape[0]
    near_out[...] = (near[...] + lefts[n:, :].astype(F32) + rights[n:, :].astype(F32)).astype(near_out.dtype)
    far_out[...] = (far[...] + far_near[...].astype(F32)).astype(far_out.dtype)


def pass_on(pieces):
    return kernel_call(pass_on_kernel, pieces, [(pieces[0].shape, BF16)] * 2, [], 4, LONG)


def finish_kernel(own, lefts, rights, far, near, out):
    n = out.shape[0]
    total = own[...] + lefts[0:n, :].astype(F32) + rights[0:n, :].astype(F32)
    out[...] = (total + far[...].astype(F32) + near[...].astype(F32)).astype(out.dtype)


def finish(pieces, said):
    return kernel_call(finish_kernel, pieces, [(pieces[0].shape, BF16)], [], 4, said)[0]


def group_sum(a):
    around = a + send(a, X_UP) + send(a, X_DOWN) + send(a, X_FAR)
    return around + send(around, Y_HI)


def on_device(student_hidden, teacher_hidden, student_head, teacher_head, sampled_ids):
    up, down, over = Link(X_UP), Link(X_DOWN), Link(Y_HI)
    half = teacher_hidden.shape[1] // 2
    t_a, t_b = teacher_hidden[:, :half], teacher_hidden[:, half:]
    left, right, near = up(student_hidden), down(student_hidden), over(student_hidden)
    ids_near = send(sampled_ids, Y_HI)
    l_a, r_a, near_a = up(t_a), down(t_a), over(after(t_a, ids_near))
    near_b = over(t_b)
    ids = kernel_call(ids_kernel, (sampled_ids, ids_near), [((1, 512), jnp.int32)], [], 1, LONG)[0]
    t_b = after(t_b, ids)
    far, right_near, left_near = up(left), down(near), over(left)
    l_b, f_a, far_near = up(t_b), down(r_a), over(far)
    ln_a, r_b, fn_a = up(near_a), down(t_b), over(f_a)
    f_b, rn_a = up(l_b), down(near_a)
    fn_b = over(f_b)
    ln_b, rn_b = up(near_b), down(near_b)

    blocks = (student_hidden, left, right, far, near, left_near, right_near, far_near)
    logits, hidden, student_stats = student_logits(ids, blocks, student_head)
    hidden_from = send(hidden, CORE)
    teacher_logits = teacher_first((t_a, l_a, r_a, f_a, near_a, ln_a, rn_a, fn_a), teacher_head)
    blocks = (t_b, l_b, r_b, f_b, near_b, ln_b, rn_b, fn_b)
    total = group_sum(teacher_second(ids, student_stats, blocks, teacher_head, teacher_logits))

    mine, other = logit_grads(ids, total, logits)
    grads = (mine, send(other, CORE), hidden, hidden_from)
    h_lefts, h_rights, h_fl = head_parts(0, ((144, BF16), (144, BF16), (72, BF16)), SHORT, *grads)
    parts = hidden_parts(ids, after(total, h_fl), logits, student_head)
    grads = (after(mine, parts[0]), *grads[1:])
    h_f, h_y, h_own = head_parts(360, ((72, F32),) * 3, SHORT, *grads)
    from_lefts, from_rights, from_fl = send(h_lefts, Z_DOWN), send(h_rights, Z_UP), send(h_fl, Y_LO)
    h_y, h_f = pass_on((h_y, h_f, from_lefts, from_rights, from_fl))
    from_y, from_f = send(h_y, Y_LO), send(h_f, Z_FAR)
    head_grad = finish((h_own, from_lefts, from_rights, from_f, from_y), SHORT)

    g_own, g_near, g_far, g_far_near, g_lefts, g_rights = parts
    from_lefts, from_rights, from_fn = send(g_lefts, X_DOWN), send(g_rights, X_UP), send(after(g_far_near, from_fl), Y_HI)
    near_sum, far_sum = pass_on((after(g_near, h_y), g_far, from_lefts, from_rights, from_fn))
    from_far, from_near = send(far_sum, X_FAR), send(near_sum, Y_HI)
    return finish((after(g_own, head_grad), from_lefts, from_rights, from_far, from_near), SHORT), head_grad


def solution(mesh):
    in_specs = (
        P(("dp", "vocab"), None),
        P(("dp", "vocab"), None),
        P("vocab", None),
        P("vocab", None),
        P("dp"),
    )
    out_specs = (P(("dp", "vocab"), None), P(("vocab", "dp"), None))
    return jax.shard_map(
        on_device, mesh=mesh, in_specs=in_specs, out_specs=out_specs, check_vma=False
    )
```

```python
import functools

import jax
import jax.numpy as jnp
from jax import lax
from jax.experimental import pallas as pl
from jax.experimental.pallas import tpu as pltpu
from jax.sharding import PartitionSpec as P

BF16 = jnp.bfloat16
F32 = jnp.float32
AXES = ("dp", "vocab")

REL = ((0, 0), (0, 1), (-1, 0), (1, 0), (-1, 1), (1, 1), (2, 0), (2, 1))


def pairs(move):
    out = []
    for i in range(128):
        dp, v = i // 8, i % 8
        y_lo, z, core, x, y_hi = dp // 8, (dp // 2) % 4, dp % 2, v // 2, v % 2
        x, y, z, core = move(x, y_hi * 2 + y_lo, z, core)
        x, y, z = x % 4, y % 4, z % 4
        out.append((i, (((y % 2) * 4 + z) * 2 + core) * 8 + x * 2 + y // 2))
    return out


X_UP = pairs(lambda x, y, z, c: (x + 1, y, z, c))
X_DOWN = pairs(lambda x, y, z, c: (x - 1, y, z, c))
X_FAR = pairs(lambda x, y, z, c: (x + 2, y, z, c))
Y_HI = pairs(lambda x, y, z, c: (x, 3 - y, z, c))
Z_UP = pairs(lambda x, y, z, c: (x, y, z + 1, c))
Z_DOWN = pairs(lambda x, y, z, c: (x, y, z - 1, c))
Z_FAR = pairs(lambda x, y, z, c: (x, y, z + 2, c))
Y_LO = pairs(lambda x, y, z, c: (x, y ^ 1, z, c))
CORE = pairs(lambda x, y, z, c: (x, y, z, 1 - c))


def send(a, to):
    return lax.ppermute(a, AXES, to)


class Link:
    def __init__(self, to, ahead=2):
        self.to, self.ahead, self.sent = to, ahead, []

    def __call__(self, a):
        if len(self.sent) >= self.ahead:
            a = after(a, self.sent[-self.ahead])
        self.sent.append(send(a, self.to))
        return self.sent[-1]


def after(a, *others):
    return lax.optimization_barrier((a, *others))[0]


def params(mib):
    return pltpu.CompilerParams(vmem_limit_bytes=mib * 2**20)


LONG, SHORT = 20, 1


VMEM = pl.BlockSpec(memory_space=pltpu.VMEM)


def kernel_call(body, arrays, outs, scratch, mib, said=SHORT):
    return pl.pallas_call(
        body,
        in_specs=[VMEM] * len(arrays),
        out_specs=[VMEM] * len(outs),
        out_shape=[jax.ShapeDtypeStruct(shape, dtype) for shape, dtype in outs],
        scratch_shapes=[pltpu.VMEM(shape, dtype) for shape, dtype in scratch],
        compiler_params=params(mib),
        cost_estimate=pl.CostEstimate(flops=said * 10**9, bytes_accessed=said * 10**6, transcendentals=0),
    )(*arrays)


class Place:
    def __init__(self):
        dp, v = lax.axis_index("dp"), lax.axis_index("vocab")
        self.y_lo, self.z, self.core = lax.div(dp, 8), lax.rem(lax.div(dp, 2), 4), lax.rem(dp, 2)
        self.vocab, self.x, self.y_hi = v, lax.div(v, 2), lax.rem(v, 2)

    def owner(self, r):
        dx, dy = REL[r]
        return lax.rem(self.x + (dx + 4), 4) * 2 + lax.rem(self.y_hi + dy, 2)

    def chip(self, dz, dy):
        return lax.rem(self.y_lo + dy, 2) * 4 + lax.rem(self.z + (dz + 4), 4)


def block(r):
    return slice(r * 64, (r + 1) * 64)


def ids_kernel(own, near, ids):
    place = Place()
    half = lax.rem(lax.div(lax.broadcasted_iota(jnp.int32, (1, 512), 1), 64), 2)
    held = jnp.where(half == place.y_hi, own[...].reshape(1, 512), near[...].reshape(1, 512))
    for r in range(8):
        ids[:, block(r)] = sum(jnp.where(place.owner(r) == a, held[:, block(a)], 0) for a in range(8))


def fold(a):
    return jnp.sum(a.reshape(a.shape[0] // 8, 8, a.shape[1]), axis=0)


NT = (((1,), (1,)), ((), ()))
NN = (((1,), (0,)), ((), ()))
TILE = 384
WIDE = 512
STATS = (8, 512)


EARLY, LATE = slice(0, 256), slice(256, 512)


def put_blocks(blocks, hidden):
    for r, rows in enumerate(blocks):
        hidden[block(r), :] = rows[...]


def sums_of(out, ids, first):
    rows = lax.broadcasted_iota(jnp.int32, out.shape, 0) + first
    return fold(jnp.exp(out)), fold(jnp.where(rows == ids, out, 0.0))


def put_stats(stats, first, tokens, sums, picks):
    stats[first:first + 1, tokens] = jnp.sum(sums, axis=0, keepdims=True)
    stats[first + 1:first + 2, tokens] = jnp.sum(picks, axis=0, keepdims=True)


def advantage(total):
    norm = jnp.log(total[0:1, :])
    return (total[3:4, :] - jnp.log(total[2:3, :])) - (total[1:2, :] - norm), norm


def tiles(head):
    return [slice(j, j + TILE) for j in range(0, head.shape[0], TILE)]


def student_kernel(ids, head, *refs):
    blocks, (logits, hidden, stats) = refs[:8], refs[8:]
    put_blocks(blocks, hidden)
    first = Place().vocab * head.shape[0]
    sums = picks = 0.0
    for tile in tiles(head):
        out = lax.dot_general(head[tile, :], hidden[...], NT, preferred_element_type=F32)
        logits[tile, :] = out
        some, pick = sums_of(out, ids[...], first + tile.start)
        sums, picks = sums + some, picks + pick
    stats[...] = jnp.zeros_like(stats)
    put_stats(stats, 0, slice(0, 512), sums, picks)


def student_logits(ids, blocks, head):
    v, d = head.shape
    outs = [((v, 512), F32), ((512, d), BF16), (STATS, F32)]
    return kernel_call(student_kernel, (ids, head, *blocks), outs, [], 6, LONG)


def teacher_early_kernel(head, *refs):
    blocks, (logits, hidden) = refs[:4], refs[4:]
    put_blocks(blocks, hidden)
    for tile in tiles(head):
        logits[tile, :] = lax.dot_general(
            head[tile, hidden.shape[1]:], hidden[...], NT, preferred_element_type=F32
        )


def teacher_early(blocks, head):
    v, d = head.shape
    return kernel_call(teacher_early_kernel, (head, *blocks), [((v, 256), F32)], [((256, d // 2), BF16)], 6, LONG)[0]


def teacher_first_kernel(ids, student_stats, early, head, *refs):
    blocks, (logits, stats, hidden) = refs[:8], refs[8:]
    put_blocks(blocks, hidden)
    first = Place().vocab * head.shape[0]
    sums = picks = 0.0
    for tile in tiles(head):
        out = lax.dot_general(head[tile, 0:hidden.shape[1]], hidden[...], NT, preferred_element_type=F32)
        logits[tile, :] = out[:, LATE]
        some, pick = sums_of(out[:, EARLY] + early[tile, :], ids[:, EARLY], first + tile.start)
        sums, picks = sums + some, picks + pick
    stats[...] = student_stats[...]
    put_stats(stats, 2, EARLY, sums, picks)


def teacher_first(ids, student_stats, early, blocks, head):
    v, d = head.shape
    arrays = (ids, student_stats, early, head, *blocks)
    return kernel_call(teacher_first_kernel, arrays, [((v, 256), F32), (STATS, F32)], [((512, d // 2), BF16)], 8, LONG)


def teacher_second_kernel(ids, first_stats, head, logits, *refs):
    blocks, (stats, hidden) = refs[:4], refs[4:]
    put_blocks(blocks, hidden)
    first = Place().vocab * head.shape[0]
    sums = picks = 0.0
    for tile in tiles(head):
        out = logits[tile, :] + lax.dot_general(
            head[tile, hidden.shape[1]:], hidden[...], NT, preferred_element_type=F32
        )
        some, pick = sums_of(out, ids[:, LATE], first + tile.start)
        sums, picks = sums + some, picks + pick
    stats[...] = first_stats[...]
    put_stats(stats, 2, LATE, sums, picks)


def teacher_second(ids, stats, blocks, head, logits):
    scratch = [((256, head.shape[1] // 2), BF16)]
    return kernel_call(teacher_second_kernel, (ids, stats, head, logits, *blocks), [(STATS, F32)], scratch, 6, LONG)[0]


def hidden_kernel(groups, places, ids, total, logits, head, *refs):
    outs, grad_t = refs[:-1], refs[-1]
    first = Place().vocab * head.shape[0]
    adv, norm = advantage(total)
    for i, start in enumerate(groups):
        tokens = slice(start, start + 128)
        for k in range(0, head.shape[0], 128):
            rows = lax.broadcasted_iota(jnp.int32, (128, 128), 0) + (first + k)
            onehot = jnp.where(rows == ids[:, tokens], 1.0, 0.0)
            part = adv[:, tokens] * (jnp.exp(logits[k:k + 128, tokens] - norm[:, tokens]) - onehot)
            grad_t[i * 128:(i + 1) * 128, k:k + 128] = part.T.astype(BF16)
    for j in range(0, head.shape[1], WIDE):
        tile = slice(j, j + WIDE)
        product = lax.dot_general(grad_t[...], head[:, tile], NN, preferred_element_type=F32)
        for r, (out, row) in enumerate(places):
            outs[out][row:row + 64, tile] = product[block(r), :].astype(outs[out].dtype)


def hidden_parts(ids, total, logits, head, groups, places, outs, said):
    v, d = head.shape
    outs = [((n, d), t) for n, t in outs]
    body = functools.partial(hidden_kernel, groups, places)
    return kernel_call(body, (ids, total, logits, head), outs, [((256, v), BF16)], 6, said)


def hidden_outer(*arrays):
    places = ((0, 0), (1, 0), (0, 64), (1, 64))
    return hidden_parts(*arrays, (128, 256), places, ((128, BF16),) * 2, LONG)


def hidden_inner(*arrays):
    places = ((0, 0), (1, 0), (2, 0), (3, 0))
    return hidden_parts(*arrays, (0, 384), places, ((64, F32),) * 3 + ((64, BF16),), SHORT)


CHIPS = ((-1, 0), (-1, 1), (1, 0), (1, 1), (2, 1), (2, 0), (0, 1), (0, 0))


def grad_kernel(ids, total, logits, mine, other, mine_f, other_f):
    place = Place()
    adv, norm = advantage(total)
    for r, chip in enumerate(CHIPS):
        for out, core in ((mine_f, place.core), (other_f, 1 - place.core)):
            start = pl.multiple_of(place.chip(*chip) * 144 + core * 72, 8)
            rows = lax.broadcasted_iota(jnp.int32, (72, 512), 0) + (place.vocab * logits.shape[0] + start)
            onehot = jnp.where(rows == ids[...], 1.0, 0.0)
            probs = jnp.exp(logits[pl.ds(start, 72), :] - norm)
            out[r * 72:(r + 1) * 72, :] = adv * (probs - onehot)
    mine[...] = mine_f[...].astype(BF16)
    other[...] = other_f[...].astype(BF16)


def logit_grads(ids, total, logits):
    half = logits.shape[0] // 2
    outs = [((half, 512), BF16)] * 2
    return kernel_call(grad_kernel, (ids, total, logits), outs, [((half, 512), F32)] * 2, 5, LONG)


def head_kernel(first, grad_mine, grad_from, hidden, hidden_from, *outs):
    n = sum(out.shape[0] for out in outs)
    rows = slice(first, first + n)
    for j in range(hidden.shape[1] // WIDE):
        tile = slice(j * WIDE, (j + 1) * WIDE)
        product = lax.dot_general(grad_mine[rows, :], hidden[:, tile], NN, preferred_element_type=F32)
        product += lax.dot_general(grad_from[rows, :], hidden_from[:, tile], NN, preferred_element_type=F32)
        start = 0
        for out in outs:
            out[:, tile] = product[start:start + out.shape[0], :].astype(out.dtype)
            start += out.shape[0]


def head_parts(first, outs, said, grad_mine, grad_from, hidden, hidden_from):
    outs = [((n, hidden.shape[1]), t) for n, t in outs]
    arrays = (grad_mine, grad_from, hidden, hidden_from)
    return kernel_call(functools.partial(head_kernel, first), arrays, outs, [], 4, said)


def pass_on_kernel(near, far, lefts, rights, far_near, near_out, far_out):
    n = near.shape[0]
    near_out[...] = (near[...] + lefts[n:, :].astype(F32) + rights[n:, :].astype(F32)).astype(near_out.dtype)
    far_out[...] = (far[...] + far_near[...].astype(F32)).astype(far_out.dtype)


def pass_on(pieces):
    return kernel_call(pass_on_kernel, pieces, [(pieces[0].shape, BF16)] * 2, [], 4, LONG)


def finish_kernel(own, lefts, rights, far, near, out):
    n = out.shape[0]
    total = own[...] + lefts[0:n, :].astype(F32) + rights[0:n, :].astype(F32)
    out[...] = (total + far[...].astype(F32) + near[...].astype(F32)).astype(out.dtype)


def finish(pieces, said):
    return kernel_call(finish_kernel, pieces, [(pieces[0].shape, BF16)], [], 4, said)[0]


def merge_kernel(shifts, *refs):
    arrays, out = refs[:-1], refs[-1]
    for r, (dx, dy) in enumerate(REL):
        total = 0.0
        for (sx, sy), a in zip(shifts, arrays):
            there = [i for i, (ox, oy) in enumerate(REL) if (ox + sx - dx) % 4 == 0 and (oy + sy - dy) % 2 == 0][0]
            total += a[:, block(there)]
        out[:, block(r)] = total


def merge(shifts, arrays):
    return kernel_call(functools.partial(merge_kernel, shifts), arrays, [(STATS, F32)], [], 2)[0]


def group_sum(a):
    around = merge(((0, 0), (-1, 0), (1, 0), (2, 0)), (a, send(a, X_UP), send(a, X_DOWN), send(a, X_FAR)))
    return merge(((0, 0), (0, 1)), (around, send(around, Y_HI)))


def on_device(student_hidden, teacher_hidden, student_head, teacher_head, sampled_ids):
    up, down, over = Link(X_UP), Link(X_DOWN), Link(Y_HI)
    half = teacher_hidden.shape[1] // 2
    t_a, t_b = teacher_hidden[:, :half], teacher_hidden[:, half:]
    left, right, near = up(student_hidden), down(student_hidden), over(student_hidden)
    ids_near = send(sampled_ids, Y_HI)
    l_a, r_a, near_a = up(t_a), down(t_a), over(after(t_a, ids_near))
    near_b = over(t_b)
    ids = kernel_call(ids_kernel, (sampled_ids, ids_near), [((1, 512), jnp.int32)], [], 1, LONG)[0]
    t_b = after(t_b, ids)
    far, right_near, left_near = up(left), down(near), over(left)
    l_b, f_a, far_near = up(t_b), down(r_a), over(far)
    ln_a, r_b, fn_a = up(near_a), down(t_b), over(f_a)
    f_b, rn_a = up(l_b), down(near_a)
    blocks = (student_hidden, near, left, right, left_near, right_near, far, far_near)
    logits, hidden, student_stats = student_logits(ids, blocks, student_head)
    fn_b = over(after(f_b, student_stats))
    ln_b, rn_b = up(near_b), down(near_b)

    hidden_from = send(hidden, CORE)
    early = teacher_early((t_b, near_b, l_b, r_b), teacher_head)
    blocks = (t_a, near_a, l_a, r_a, ln_a, rn_a, f_a, fn_a)
    teacher_logits, stats = teacher_first(ids, student_stats, early, blocks, teacher_head)
    total = group_sum(teacher_second(ids, stats, (ln_b, rn_b, f_b, fn_b), teacher_head, teacher_logits))

    mine, other = logit_grads(ids, total, logits)
    grads = (mine, send(other, CORE), hidden, hidden_from)
    h_lefts, h_rights, h_fl = head_parts(0, ((144, BF16), (144, BF16), (72, BF16)), SHORT, *grads)
    g_lefts, g_rights = hidden_outer(ids, after(total, h_fl), logits, student_head)
    from_fl = send(h_fl, Y_LO)
    g_own, g_near, g_far, g_far_near = hidden_inner(ids, after(total, from_fl), logits, student_head)
    grads = (after(mine, g_lefts), *grads[1:])
    h_f, h_y, h_own = head_parts(360, ((72, F32),) * 3, SHORT, *grads)
    from_lefts, from_rights = send(h_lefts, Z_DOWN), send(h_rights, Z_UP)
    h_y, h_f = pass_on((h_y, h_f, from_lefts, from_rights, from_fl))
    from_y, from_f = send(h_y, Y_LO), send(h_f, Z_FAR)
    head_grad = finish((h_own, from_lefts, from_rights, from_f, from_y), SHORT)

    from_lefts, from_rights, from_fn = send(g_lefts, X_DOWN), send(g_rights, X_UP), send(after(g_far_near, from_fl), Y_HI)
    near_sum, far_sum = pass_on((after(g_near, h_y), g_far, from_lefts, from_rights, from_fn))
    from_far, from_near = send(far_sum, X_FAR), send(near_sum, Y_HI)
    return finish((after(g_own, head_grad), from_lefts, from_rights, from_far, from_near), SHORT), head_grad


def solution(mesh):
    in_specs = (
        P(("dp", "vocab"), None),
        P(("dp", "vocab"), None),
        P("vocab", None),
        P("vocab", None),
        P("dp"),
    )
    out_specs = (P(("dp", "vocab"), None), P(("vocab", "dp"), None))
    return jax.shard_map(
        on_device, mesh=mesh, in_specs=in_specs, out_specs=out_specs, check_vma=False
    )
```

```python
import functools

import jax
import jax.numpy as jnp
from jax import lax
from jax.experimental import pallas as pl
from jax.experimental.pallas import tpu as pltpu
from jax.sharding import PartitionSpec as P

BF16 = jnp.bfloat16
F32 = jnp.float32
AXES = ("dp", "vocab")

REL = ((0, 0), (0, 1), (-1, 0), (1, 0), (-1, 1), (1, 1), (2, 0), (2, 1))


def pairs(move):
    out = []
    for i in range(128):
        dp, v = i // 8, i % 8
        y_lo, z, core, x, y_hi = dp // 8, (dp // 2) % 4, dp % 2, v // 2, v % 2
        x, y, z, core = move(x, y_hi * 2 + y_lo, z, core)
        x, y, z = x % 4, y % 4, z % 4
        out.append((i, (((y % 2) * 4 + z) * 2 + core) * 8 + x * 2 + y // 2))
    return out


X_UP = pairs(lambda x, y, z, c: (x + 1, y, z, c))
X_DOWN = pairs(lambda x, y, z, c: (x - 1, y, z, c))
X_FAR = pairs(lambda x, y, z, c: (x + 2, y, z, c))
Y_HI = pairs(lambda x, y, z, c: (x, 3 - y, z, c))
Z_UP = pairs(lambda x, y, z, c: (x, y, z + 1, c))
Z_DOWN = pairs(lambda x, y, z, c: (x, y, z - 1, c))
Z_FAR = pairs(lambda x, y, z, c: (x, y, z + 2, c))
Y_LO = pairs(lambda x, y, z, c: (x, y ^ 1, z, c))
CORE = pairs(lambda x, y, z, c: (x, y, z, 1 - c))


def send(a, to):
    return lax.ppermute(a, AXES, to)


class Link:
    def __init__(self, to, ahead=2):
        self.to, self.ahead, self.sent = to, ahead, []

    def __call__(self, a):
        if len(self.sent) >= self.ahead:
            a = after(a, self.sent[-self.ahead])
        self.sent.append(send(a, self.to))
        return self.sent[-1]


def after(a, *others):
    return lax.optimization_barrier((a, *others))[0]


def params(mib):
    return pltpu.CompilerParams(vmem_limit_bytes=mib * 2**20)


LONG, SHORT = 20, 1


VMEM = pl.BlockSpec(memory_space=pltpu.VMEM)


def kernel_call(body, arrays, outs, scratch, mib, said=SHORT):
    return pl.pallas_call(
        body,
        in_specs=[VMEM] * len(arrays),
        out_specs=[VMEM] * len(outs),
        out_shape=[jax.ShapeDtypeStruct(shape, dtype) for shape, dtype in outs],
        scratch_shapes=[pltpu.VMEM(shape, dtype) for shape, dtype in scratch],
        compiler_params=params(mib),
        cost_estimate=pl.CostEstimate(flops=said * 10**9, bytes_accessed=said * 10**6, transcendentals=0),
    )(*arrays)


class Place:
    def __init__(self):
        dp, v = lax.axis_index("dp"), lax.axis_index("vocab")
        self.y_lo, self.z, self.core = lax.div(dp, 8), lax.rem(lax.div(dp, 2), 4), lax.rem(dp, 2)
        self.vocab, self.x, self.y_hi = v, lax.div(v, 2), lax.rem(v, 2)

    def owner(self, r):
        dx, dy = REL[r]
        return lax.rem(self.x + (dx + 4), 4) * 2 + lax.rem(self.y_hi + dy, 2)

    def chip(self, dz, dy):
        return lax.rem(self.y_lo + dy, 2) * 4 + lax.rem(self.z + (dz + 4), 4)


def block(r):
    return slice(r * 64, (r + 1) * 64)


def ids_kernel(own, near, ids):
    place = Place()
    half = lax.rem(lax.div(lax.broadcasted_iota(jnp.int32, (1, 512), 1), 64), 2)
    held = jnp.where(half == place.y_hi, own[...].reshape(1, 512), near[...].reshape(1, 512))
    for r in range(8):
        ids[:, block(r)] = sum(jnp.where(place.owner(r) == a, held[:, block(a)], 0) for a in range(8))


def fold(a):
    return jnp.sum(a.reshape(a.shape[0] // 8, 8, a.shape[1]), axis=0)


NT = (((1,), (1,)), ((), ()))
NN = (((1,), (0,)), ((), ()))
TILE = 384
WIDE = 512
STATS = (8, 512)


EARLY, LATE = slice(0, 256), slice(256, 512)


def put_blocks(blocks, hidden):
    for r, rows in enumerate(blocks):
        hidden[block(r), :] = rows[...]


def sums_of(out, ids, first):
    rows = lax.broadcasted_iota(jnp.int32, out.shape, 0) + first
    return fold(jnp.exp(out)), fold(jnp.where(rows == ids, out, 0.0))


def put_stats(stats, first, tokens, sums, picks):
    stats[first:first + 1, tokens] = jnp.sum(sums, axis=0, keepdims=True)
    stats[first + 1:first + 2, tokens] = jnp.sum(picks, axis=0, keepdims=True)


def advantage(total):
    norm = jnp.log(total[0:1, :])
    return (total[3:4, :] - jnp.log(total[2:3, :])) - (total[1:2, :] - norm), norm


def tiles(head):
    return [slice(j, j + TILE) for j in range(0, head.shape[0], TILE)]


def student_kernel(ids, head, *refs):
    blocks, (logits, hidden, stats) = refs[:8], refs[8:]
    put_blocks(blocks, hidden)
    first = Place().vocab * head.shape[0]
    sums = picks = 0.0
    for tile in tiles(head):
        out = lax.dot_general(head[tile, :], hidden[...], NT, preferred_element_type=F32)
        logits[tile, :] = out
        some, pick = sums_of(out, ids[...], first + tile.start)
        sums, picks = sums + some, picks + pick
    stats[...] = jnp.zeros_like(stats)
    put_stats(stats, 0, slice(0, 512), sums, picks)


def student_logits(ids, blocks, head):
    v, d = head.shape
    outs = [((v, 512), F32), ((512, d), BF16), (STATS, F32)]
    return kernel_call(student_kernel, (ids, head, *blocks), outs, [], 6, LONG)


def teacher_early_kernel(head, *refs):
    blocks, (logits, hidden) = refs[:4], refs[4:]
    put_blocks(blocks, hidden)
    for tile in tiles(head):
        logits[tile, :] = lax.dot_general(
            head[tile, hidden.shape[1]:], hidden[...], NT, preferred_element_type=F32
        )


def teacher_early(blocks, head):
    v, d = head.shape
    return kernel_call(teacher_early_kernel, (head, *blocks), [((v, 256), F32)], [((256, d // 2), BF16)], 6, LONG)[0]


def teacher_first_kernel(ids, student_stats, early, head, *refs):
    blocks, (logits, stats, hidden) = refs[:8], refs[8:]
    put_blocks(blocks, hidden)
    first = Place().vocab * head.shape[0]
    sums = picks = 0.0
    for tile in tiles(head):
        out = lax.dot_general(head[tile, 0:hidden.shape[1]], hidden[...], NT, preferred_element_type=F32)
        logits[tile, :] = out[:, LATE]
        some, pick = sums_of(out[:, EARLY] + early[tile, :], ids[:, EARLY], first + tile.start)
        sums, picks = sums + some, picks + pick
    stats[...] = student_stats[...]
    put_stats(stats, 2, EARLY, sums, picks)


def teacher_first(ids, student_stats, early, blocks, head):
    v, d = head.shape
    arrays = (ids, student_stats, early, head, *blocks)
    return kernel_call(teacher_first_kernel, arrays, [((v, 256), F32), (STATS, F32)], [((512, d // 2), BF16)], 8, LONG)


def teacher_second_kernel(ids, first_stats, head, logits, *refs):
    blocks, (stats, hidden) = refs[:4], refs[4:]
    put_blocks(blocks, hidden)
    first = Place().vocab * head.shape[0]
    sums = picks = 0.0
    for tile in tiles(head):
        out = logits[tile, :] + lax.dot_general(
            head[tile, hidden.shape[1]:], hidden[...], NT, preferred_element_type=F32
        )
        some, pick = sums_of(out, ids[:, LATE], first + tile.start)
        sums, picks = sums + some, picks + pick
    stats[...] = first_stats[...]
    put_stats(stats, 2, LATE, sums, picks)


def teacher_second(ids, stats, blocks, head, logits):
    scratch = [((256, head.shape[1] // 2), BF16)]
    return kernel_call(teacher_second_kernel, (ids, stats, head, logits, *blocks), [(STATS, F32)], scratch, 6, LONG)[0]


def hidden_kernel(groups, places, ids, total, logits, head, *refs):
    outs, grad_t = refs[:-1], refs[-1]
    first = Place().vocab * head.shape[0]
    adv, norm = advantage(total)
    for i, start in enumerate(groups):
        tokens = slice(start, start + 128)
        for k in range(0, head.shape[0], 128):
            rows = lax.broadcasted_iota(jnp.int32, (128, 128), 0) + (first + k)
            onehot = jnp.where(rows == ids[:, tokens], 1.0, 0.0)
            part = adv[:, tokens] * (jnp.exp(logits[k:k + 128, tokens] - norm[:, tokens]) - onehot)
            grad_t[i * 128:(i + 1) * 128, k:k + 128] = part.T.astype(BF16)
    for j in range(0, head.shape[1], WIDE):
        tile = slice(j, j + WIDE)
        product = lax.dot_general(grad_t[...], head[:, tile], NN, preferred_element_type=F32)
        for r, (out, row) in enumerate(places):
            outs[out][row:row + 64, tile] = product[block(r), :].astype(outs[out].dtype)


def hidden_parts(ids, total, logits, head, groups, places, outs, said):
    v, d = head.shape
    outs = [((n, d), t) for n, t in outs]
    body = functools.partial(hidden_kernel, groups, places)
    return kernel_call(body, (ids, total, logits, head), outs, [((256, v), BF16)], 6, said)


def hidden_outer(*arrays):
    places = ((0, 0), (1, 0), (0, 64), (1, 64))
    return hidden_parts(*arrays, (128, 256), places, ((128, BF16),) * 2, LONG)


def hidden_inner(*arrays):
    places = ((0, 0), (1, 0), (2, 0), (3, 0))
    return hidden_parts(*arrays, (0, 384), places, ((64, F32),) * 3 + ((64, BF16),), SHORT)


CHIPS = ((-1, 0), (-1, 1), (1, 0), (1, 1), (2, 1), (2, 0), (0, 1), (0, 0))


def grad_kernel(ids, total, logits, mine, other, mine_f, other_f):
    place = Place()
    adv, norm = advantage(total)
    for r, chip in enumerate(CHIPS):
        for out, core in ((mine_f, place.core), (other_f, 1 - place.core)):
            start = pl.multiple_of(place.chip(*chip) * 144 + core * 72, 8)
            rows = lax.broadcasted_iota(jnp.int32, (72, 512), 0) + (place.vocab * logits.shape[0] + start)
            onehot = jnp.where(rows == ids[...], 1.0, 0.0)
            probs = jnp.exp(logits[pl.ds(start, 72), :] - norm)
            out[r * 72:(r + 1) * 72, :] = adv * (probs - onehot)
    mine[...] = mine_f[...].astype(BF16)
    other[...] = other_f[...].astype(BF16)


def logit_grads(ids, total, logits):
    half = logits.shape[0] // 2
    outs = [((half, 512), BF16)] * 2
    return kernel_call(grad_kernel, (ids, total, logits), outs, [((half, 512), F32)] * 2, 5, LONG)


def head_own_kernel(grad, hidden, out):
    for j in range(0, hidden.shape[1], WIDE):
        tile = slice(j, j + WIDE)
        out[:, tile] = lax.dot_general(grad[...], hidden[:, tile], NN, preferred_element_type=F32)


def head_own(grad, hidden):
    outs = [((grad.shape[0], hidden.shape[1]), F32)]
    return kernel_call(head_own_kernel, (grad, hidden), outs, [], 4)[0]


def head_kernel(first, grad, hidden, own, *outs):
    n = sum(out.shape[0] for out in outs)
    rows = slice(first, first + n)
    for j in range(0, hidden.shape[1], WIDE):
        tile = slice(j, j + WIDE)
        product = own[rows, tile] + lax.dot_general(grad[rows, :], hidden[:, tile], NN, preferred_element_type=F32)
        start = 0
        for out in outs:
            out[:, tile] = product[start:start + out.shape[0], :].astype(out.dtype)
            start += out.shape[0]


def head_parts(first, outs, grad, hidden, own):
    outs = [((n, hidden.shape[1]), t) for n, t in outs]
    return kernel_call(functools.partial(head_kernel, first), (grad, hidden, own), outs, [], 4)


def pass_on_kernel(near, far, lefts, rights, far_near, near_out, far_out):
    n = near.shape[0]
    near_out[...] = (near[...] + lefts[n:, :].astype(F32) + rights[n:, :].astype(F32)).astype(near_out.dtype)
    far_out[...] = (far[...] + far_near[...].astype(F32)).astype(far_out.dtype)


def pass_on(pieces):
    return kernel_call(pass_on_kernel, pieces, [(pieces[0].shape, BF16)] * 2, [], 4, LONG)


def finish_kernel(own, lefts, rights, far, near, out):
    n = out.shape[0]
    total = own[...] + lefts[0:n, :].astype(F32) + rights[0:n, :].astype(F32)
    out[...] = (total + far[...].astype(F32) + near[...].astype(F32)).astype(out.dtype)


def finish(pieces, said):
    return kernel_call(finish_kernel, pieces, [(pieces[0].shape, BF16)], [], 4, said)[0]


def merge_kernel(shifts, *refs):
    arrays, out = refs[:-1], refs[-1]
    for r, (dx, dy) in enumerate(REL):
        total = 0.0
        for (sx, sy), a in zip(shifts, arrays):
            there = [i for i, (ox, oy) in enumerate(REL) if (ox + sx - dx) % 4 == 0 and (oy + sy - dy) % 2 == 0][0]
            total += a[:, block(there)]
        out[:, block(r)] = total


def merge(shifts, arrays):
    return kernel_call(functools.partial(merge_kernel, shifts), arrays, [(STATS, F32)], [], 2)[0]


def group_sum(a):
    around = merge(((0, 0), (-1, 0), (1, 0), (2, 0)), (a, send(a, X_UP), send(a, X_DOWN), send(a, X_FAR)))
    return merge(((0, 0), (0, 1)), (around, send(around, Y_HI)))


def on_device(student_hidden, teacher_hidden, student_head, teacher_head, sampled_ids):
    up, down, over = Link(X_UP), Link(X_DOWN), Link(Y_HI)
    half = teacher_hidden.shape[1] // 2
    t_a, t_b = teacher_hidden[:, :half], teacher_hidden[:, half:]
    t_b0 = t_b
    left = up(student_hidden)
    right = down(student_hidden)
    near = over(student_hidden)
    ids_near = send(sampled_ids, Y_HI)
    ids = kernel_call(ids_kernel, (sampled_ids, ids_near), [((1, 512), jnp.int32)], [], 1, LONG)[0]
    t_b0, t_b = t_b, after(t_b, ids)
    l_b = up(t_b)
    r_a = down(t_a)
    near_a = over(after(t_a, ids_near))
    far = up(left)
    right_near = down(near)
    near_b = over(t_b0)
    l_a = up(t_a)
    f_a = down(r_a)
    left_near = over(left)
    f_b = up(l_b)
    r_b = down(t_b)
    far_near = over(far)
    ln_a = up(near_a)
    rn_a = down(near_a)
    fn_a = over(f_a)

    blocks = (student_hidden, near, left, right, left_near, right_near, far, far_near)
    logits, hidden, student_stats = student_logits(ids, blocks, student_head)
    fn_b = over(after(f_b, student_stats))
    ln_b = up(near_b)
    rn_b = down(near_b)

    hidden_from = send(hidden, CORE)
    early = teacher_early((t_b, near_b, l_b, r_b), teacher_head)
    blocks = (t_a, near_a, l_a, r_a, ln_a, rn_a, f_a, fn_a)
    teacher_logits, stats = teacher_first(ids, student_stats, early, blocks, teacher_head)
    total = group_sum(teacher_second(ids, stats, (ln_b, rn_b, f_b, fn_b), teacher_head, teacher_logits))

    mine, other = logit_grads(ids, total, logits)
    grad_from, sums = send(other, CORE), head_own(mine, hidden)
    h_lefts, h_rights, h_fl = head_parts(0, ((144, BF16), (144, BF16), (72, BF16)), grad_from, hidden_from, sums)
    g_lefts, g_rights = hidden_outer(ids, after(total, h_fl), logits, student_head)
    from_fl = send(h_fl, Y_LO)
    g_own, g_near, g_far, g_far_near = hidden_inner(ids, after(total, from_fl), logits, student_head)
    h_f, h_y, h_own = head_parts(360, ((72, F32),) * 3, after(grad_from, g_lefts), hidden_from, sums)
    from_lefts, from_rights = send(h_lefts, Z_DOWN), send(h_rights, Z_UP)
    h_y, h_f = pass_on((h_y, h_f, from_lefts, from_rights, from_fl))
    from_y, from_f = send(h_y, Y_LO), send(h_f, Z_FAR)
    head_grad = finish((h_own, from_lefts, from_rights, from_f, from_y), SHORT)

    from_lefts, from_rights, from_fn = send(g_lefts, X_DOWN), send(g_rights, X_UP), send(after(g_far_near, from_fl), Y_HI)
    near_sum, far_sum = pass_on((after(g_near, h_y), g_far, from_lefts, from_rights, from_fn))
    from_far, from_near = send(far_sum, X_FAR), send(near_sum, Y_HI)
    return finish((after(g_own, head_grad), from_lefts, from_rights, from_far, from_near), SHORT), head_grad


def solution(mesh):
    in_specs = (
        P(("dp", "vocab"), None),
        P(("dp", "vocab"), None),
        P("vocab", None),
        P("vocab", None),
        P("dp"),
    )
    out_specs = (P(("dp", "vocab"), None), P(("vocab", "dp"), None))
    return jax.shard_map(
        on_device, mesh=mesh, in_specs=in_specs, out_specs=out_specs, check_vma=False
    )
```

```python
import functools

import jax
import jax.numpy as jnp
from jax import lax
from jax.experimental import pallas as pl
from jax.experimental.pallas import tpu as pltpu
from jax.sharding import PartitionSpec as P

BF16 = jnp.bfloat16
F32 = jnp.float32
AXES = ("dp", "vocab")

REL = ((0, 0), (0, 1), (-1, 0), (1, 0), (-1, 1), (1, 1), (2, 0), (2, 1))


def pairs(move):
    out = []
    for i in range(128):
        dp, v = i // 8, i % 8
        y_lo, z, core, x, y_hi = dp // 8, (dp // 2) % 4, dp % 2, v // 2, v % 2
        x, y, z, core = move(x, y_hi * 2 + y_lo, z, core)
        x, y, z = x % 4, y % 4, z % 4
        out.append((i, (((y % 2) * 4 + z) * 2 + core) * 8 + x * 2 + y // 2))
    return out


X_UP = pairs(lambda x, y, z, c: (x + 1, y, z, c))
X_DOWN = pairs(lambda x, y, z, c: (x - 1, y, z, c))
X_FAR = pairs(lambda x, y, z, c: (x + 2, y, z, c))
Y_HI = pairs(lambda x, y, z, c: (x, 3 - y, z, c))
Z_UP = pairs(lambda x, y, z, c: (x, y, z + 1, c))
Z_DOWN = pairs(lambda x, y, z, c: (x, y, z - 1, c))
Z_FAR = pairs(lambda x, y, z, c: (x, y, z + 2, c))
Y_LO = pairs(lambda x, y, z, c: (x, y ^ 1, z, c))
CORE = pairs(lambda x, y, z, c: (x, y, z, 1 - c))


def send(a, to):
    return lax.ppermute(a, AXES, to)


class Link:
    def __init__(self, to, ahead=2):
        self.to, self.ahead, self.sent = to, ahead, []

    def __call__(self, a):
        if len(self.sent) >= self.ahead:
            a = after(a, self.sent[-self.ahead])
        self.sent.append(send(a, self.to))
        return self.sent[-1]


def after(a, *others):
    return lax.optimization_barrier((a, *others))[0]


def params(mib):
    return pltpu.CompilerParams(vmem_limit_bytes=mib * 2**20)


LONG, SHORT = 20, 1


VMEM = pl.BlockSpec(memory_space=pltpu.VMEM)


def kernel_call(body, arrays, outs, scratch, mib, said=SHORT):
    return pl.pallas_call(
        body,
        in_specs=[VMEM] * len(arrays),
        out_specs=[VMEM] * len(outs),
        out_shape=[jax.ShapeDtypeStruct(shape, dtype) for shape, dtype in outs],
        scratch_shapes=[pltpu.VMEM(shape, dtype) for shape, dtype in scratch],
        compiler_params=params(mib),
        cost_estimate=pl.CostEstimate(flops=said * 10**9, bytes_accessed=said * 10**6, transcendentals=0),
    )(*arrays)


class Place:
    def __init__(self):
        dp, v = lax.axis_index("dp"), lax.axis_index("vocab")
        self.y_lo, self.z, self.core = lax.div(dp, 8), lax.rem(lax.div(dp, 2), 4), lax.rem(dp, 2)
        self.vocab, self.x, self.y_hi = v, lax.div(v, 2), lax.rem(v, 2)

    def owner(self, r):
        dx, dy = REL[r]
        return lax.rem(self.x + (dx + 4), 4) * 2 + lax.rem(self.y_hi + dy, 2)

    def chip(self, dz, dy):
        return lax.rem(self.y_lo + dy, 2) * 4 + lax.rem(self.z + (dz + 4), 4)


def block(r):
    return slice(r * 64, (r + 1) * 64)


def ids_kernel(own, near, ids):
    place = Place()
    half = lax.rem(lax.div(lax.broadcasted_iota(jnp.int32, (1, 512), 1), 64), 2)
    held = jnp.where(half == place.y_hi, own[...].reshape(1, 512), near[...].reshape(1, 512))
    for r in range(8):
        ids[:, block(r)] = sum(jnp.where(place.owner(r) == a, held[:, block(a)], 0) for a in range(8))


def fold(a):
    return jnp.sum(a.reshape(a.shape[0] // 8, 8, a.shape[1]), axis=0)


NT = (((1,), (1,)), ((), ()))
NN = (((1,), (0,)), ((), ()))
TILE = 384
WIDE = 512
STATS = (8, 512)


EARLY, LATE = slice(0, 256), slice(256, 512)


def put_blocks(blocks, hidden):
    for r, rows in enumerate(blocks):
        hidden[block(r), :] = rows[...]


def sums_of(out, ids, first):
    rows = lax.broadcasted_iota(jnp.int32, out.shape, 0) + first
    return fold(jnp.exp(out)), fold(jnp.where(rows == ids, out, 0.0))


def put_stats(stats, first, tokens, sums, picks):
    stats[first:first + 1, tokens] = jnp.sum(sums, axis=0, keepdims=True)
    stats[first + 1:first + 2, tokens] = jnp.sum(picks, axis=0, keepdims=True)


def advantage(total):
    norm = jnp.log(total[0:1, :])
    return (total[3:4, :] - jnp.log(total[2:3, :])) - (total[1:2, :] - norm), norm


def tiles(head):
    return [slice(j, j + TILE) for j in range(0, head.shape[0], TILE)]


def student_kernel(ids, head, *refs):
    blocks, (logits, hidden, stats) = refs[:8], refs[8:]
    put_blocks(blocks, hidden)
    first = Place().vocab * head.shape[0]
    sums = picks = 0.0
    for tile in tiles(head):
        out = lax.dot_general(head[tile, :], hidden[...], NT, preferred_element_type=F32)
        logits[tile, :] = out
        some, pick = sums_of(out, ids[...], first + tile.start)
        sums, picks = sums + some, picks + pick
    stats[...] = jnp.zeros_like(stats)
    put_stats(stats, 0, slice(0, 512), sums, picks)


def student_logits(ids, blocks, head):
    v, d = head.shape
    outs = [((v, 512), F32), ((512, d), BF16), (STATS, F32)]
    return kernel_call(student_kernel, (ids, head, *blocks), outs, [], 6, LONG)


def teacher_early_kernel(head, *refs):
    blocks, (logits, hidden) = refs[:4], refs[4:]
    put_blocks(blocks, hidden)
    for tile in tiles(head):
        logits[tile, :] = lax.dot_general(
            head[tile, hidden.shape[1]:], hidden[...], NT, preferred_element_type=F32
        )


def teacher_early(blocks, head):
    v, d = head.shape
    return kernel_call(teacher_early_kernel, (head, *blocks), [((v, 256), F32)], [((256, d // 2), BF16)], 6, LONG)[0]


def teacher_first_kernel(ids, student_stats, early, head, *refs):
    blocks, (logits, stats, hidden) = refs[:8], refs[8:]
    put_blocks(blocks, hidden)
    first = Place().vocab * head.shape[0]
    sums = picks = 0.0
    for tile in tiles(head):
        out = lax.dot_general(head[tile, 0:hidden.shape[1]], hidden[...], NT, preferred_element_type=F32)
        logits[tile, :] = out[:, LATE]
        some, pick = sums_of(out[:, EARLY] + early[tile, :], ids[:, EARLY], first + tile.start)
        sums, picks = sums + some, picks + pick
    stats[...] = student_stats[...]
    put_stats(stats, 2, EARLY, sums, picks)


def teacher_first(ids, student_stats, early, blocks, head):
    v, d = head.shape
    arrays = (ids, student_stats, early, head, *blocks)
    return kernel_call(teacher_first_kernel, arrays, [((v, 256), F32), (STATS, F32)], [((512, d // 2), BF16)], 8, LONG)


def teacher_second_kernel(ids, first_stats, head, logits, *refs):
    blocks, (stats, hidden) = refs[:4], refs[4:]
    put_blocks(blocks, hidden)
    first = Place().vocab * head.shape[0]
    sums = picks = 0.0
    for tile in tiles(head):
        out = logits[tile, :] + lax.dot_general(
            head[tile, hidden.shape[1]:], hidden[...], NT, preferred_element_type=F32
        )
        some, pick = sums_of(out, ids[:, LATE], first + tile.start)
        sums, picks = sums + some, picks + pick
    stats[...] = first_stats[...]
    put_stats(stats, 2, LATE, sums, picks)


def teacher_second(ids, stats, blocks, head, logits):
    scratch = [((256, head.shape[1] // 2), BF16)]
    return kernel_call(teacher_second_kernel, (ids, stats, head, logits, *blocks), [(STATS, F32)], scratch, 6, LONG)[0]


def hidden_kernel(groups, places, ids, total, logits, head, *refs):
    outs, grad_t = refs[:-1], refs[-1]
    first = Place().vocab * head.shape[0]
    adv, norm = advantage(total)
    for i, start in enumerate(groups):
        tokens = slice(start, start + 128)
        for k in range(0, head.shape[0], 128):
            rows = lax.broadcasted_iota(jnp.int32, (128, 128), 0) + (first + k)
            onehot = jnp.where(rows == ids[:, tokens], 1.0, 0.0)
            part = adv[:, tokens] * (jnp.exp(logits[k:k + 128, tokens] - norm[:, tokens]) - onehot)
            grad_t[i * 128:(i + 1) * 128, k:k + 128] = part.T.astype(BF16)
    for j in range(0, head.shape[1], WIDE):
        tile = slice(j, j + WIDE)
        product = lax.dot_general(grad_t[...], head[:, tile], NN, preferred_element_type=F32)
        for r, (out, row) in enumerate(places):
            outs[out][row:row + 64, tile] = product[block(r), :].astype(outs[out].dtype)


def hidden_parts(ids, total, logits, head, groups, places, outs, said):
    v, d = head.shape
    outs = [((n, d), t) for n, t in outs]
    body = functools.partial(hidden_kernel, groups, places)
    return kernel_call(body, (ids, total, logits, head), outs, [((256, v), BF16)], 6, said)


def hidden_outer(*arrays):
    places = ((0, 0), (1, 0), (0, 64), (1, 64))
    return hidden_parts(*arrays, (128, 256), places, ((128, BF16),) * 2, LONG)


def hidden_inner(*arrays):
    places = ((0, 0), (1, 0), (2, 0), (3, 0))
    return hidden_parts(*arrays, (0, 384), places, ((64, F32),) * 3 + ((64, BF16),), SHORT)


CHIPS = ((-1, 0), (-1, 1), (1, 0), (1, 1), (2, 1), (2, 0), (0, 1), (0, 0))


def grad_kernel(ids, total, logits, mine, other, mine_f, other_f):
    place = Place()
    adv, norm = advantage(total)
    for r, chip in enumerate(CHIPS):
        for out, core in ((mine_f, place.core), (other_f, 1 - place.core)):
            start = pl.multiple_of(place.chip(*chip) * 144 + core * 72, 8)
            rows = lax.broadcasted_iota(jnp.int32, (72, 512), 0) + (place.vocab * logits.shape[0] + start)
            onehot = jnp.where(rows == ids[...], 1.0, 0.0)
            probs = jnp.exp(logits[pl.ds(start, 72), :] - norm)
            out[r * 72:(r + 1) * 72, :] = adv * (probs - onehot)
    mine[...] = mine_f[...].astype(BF16)
    other[...] = other_f[...].astype(BF16)


def logit_grads(ids, total, logits):
    half = logits.shape[0] // 2
    outs = [((half, 512), BF16)] * 2
    return kernel_call(grad_kernel, (ids, total, logits), outs, [((half, 512), F32)] * 2, 5, LONG)


def head_own_kernel(grad, hidden, out):
    for j in range(0, hidden.shape[1], WIDE):
        tile = slice(j, j + WIDE)
        out[:, tile] = lax.dot_general(grad[...], hidden[:, tile], NN, preferred_element_type=F32)


def head_own(grad, hidden):
    outs = [((grad.shape[0], hidden.shape[1]), F32)]
    return kernel_call(head_own_kernel, (grad, hidden), outs, [], 4)[0]


def head_kernel(first, grad, hidden, own, *outs):
    n = sum(out.shape[0] for out in outs)
    rows = slice(first, first + n)
    for j in range(0, hidden.shape[1], WIDE):
        tile = slice(j, j + WIDE)
        product = own[rows, tile] + lax.dot_general(grad[rows, :], hidden[:, tile], NN, preferred_element_type=F32)
        start = 0
        for out in outs:
            out[:, tile] = product[start:start + out.shape[0], :].astype(out.dtype)
            start += out.shape[0]


def head_parts(first, outs, grad, hidden, own):
    outs = [((n, hidden.shape[1]), t) for n, t in outs]
    return kernel_call(functools.partial(head_kernel, first), (grad, hidden, own), outs, [], 4)


def pass_on_kernel(near, far, lefts, rights, far_near, near_out, far_out):
    n = near.shape[0]
    near_out[...] = (near[...] + lefts[n:, :].astype(F32) + rights[n:, :].astype(F32)).astype(near_out.dtype)
    far_out[...] = (far[...] + far_near[...].astype(F32)).astype(far_out.dtype)


def pass_on(pieces):
    return kernel_call(pass_on_kernel, pieces, [(pieces[0].shape, BF16)] * 2, [], 4, LONG)


def finish_kernel(own, lefts, rights, far, near, out):
    n = out.shape[0]
    total = own[...] + lefts[0:n, :].astype(F32) + rights[0:n, :].astype(F32)
    out[...] = (total + far[...].astype(F32) + near[...].astype(F32)).astype(out.dtype)


def finish(pieces, said):
    return kernel_call(finish_kernel, pieces, [(pieces[0].shape, BF16)], [], 4, said)[0]


def merge_kernel(shifts, *refs):
    arrays, out = refs[:-1], refs[-1]
    for r, (dx, dy) in enumerate(REL):
        total = 0.0
        for (sx, sy), a in zip(shifts, arrays):
            there = [i for i, (ox, oy) in enumerate(REL) if (ox + sx - dx) % 4 == 0 and (oy + sy - dy) % 2 == 0][0]
            total += a[:, block(there)]
        out[:, block(r)] = total


def merge(shifts, arrays):
    return kernel_call(functools.partial(merge_kernel, shifts), arrays, [(STATS, F32)], [], 2)[0]


def group_sum(a):
    around = merge(((0, 0), (-1, 0), (1, 0), (2, 0)), (a, send(a, X_UP), send(a, X_DOWN), send(a, X_FAR)))
    return merge(((0, 0), (0, 1)), (around, send(around, Y_HI)))


def on_device(student_hidden, teacher_hidden, student_head, teacher_head, sampled_ids):
    up, down, over = Link(X_UP), Link(X_DOWN), Link(Y_HI)
    half = teacher_hidden.shape[1] // 2
    t_a, t_b = teacher_hidden[:, :half], teacher_hidden[:, half:]
    t_b0 = t_b
    left = up(student_hidden)
    right = down(student_hidden)
    near = over(student_hidden)
    ids_near = send(sampled_ids, Y_HI)
    ids = kernel_call(ids_kernel, (sampled_ids, ids_near), [((1, 512), jnp.int32)], [], 1, LONG)[0]
    t_b0, t_b = t_b, after(t_b, ids)
    l_b = up(t_b)
    r_a = down(t_a)
    near_a = over(after(t_a, ids_near))
    far = up(left)
    right_near = down(near)
    near_b = over(t_b0)
    l_a = up(t_a)
    f_a = down(r_a)
    left_near = over(left)
    f_b = up(l_b)
    r_b = down(t_b)
    far_near = over(far)
    ln_a = up(near_a)
    rn_a = down(near_a)
    fn_a = over(f_a)

    blocks = (student_hidden, near, left, right, left_near, right_near, far, far_near)
    logits, hidden, student_stats = student_logits(after(ids, rn_a), blocks, student_head)
    fn_b = over(f_b)
    ln_b = up(near_b)
    rn_b = down(near_b)

    hidden_from = send(hidden, CORE)
    early = teacher_early((t_b, near_b, l_b, r_b), teacher_head)
    blocks = (t_a, near_a, l_a, r_a, ln_a, rn_a, f_a, fn_a)
    teacher_logits, stats = teacher_first(ids, student_stats, early, blocks, teacher_head)
    total = group_sum(teacher_second(ids, stats, (ln_b, rn_b, f_b, fn_b), teacher_head, teacher_logits))

    mine, other = logit_grads(ids, total, logits)
    grad_from, sums = send(other, CORE), head_own(mine, hidden)
    h_lefts, h_rights, h_fl = head_parts(0, ((144, BF16), (144, BF16), (72, BF16)), grad_from, hidden_from, sums)
    g_lefts, g_rights = hidden_outer(ids, after(total, h_fl), logits, student_head)
    from_fl = send(h_fl, Y_LO)
    g_own, g_near, g_far, g_far_near = hidden_inner(ids, after(total, from_fl), logits, student_head)
    h_f, h_y, h_own = head_parts(360, ((72, F32),) * 3, after(grad_from, g_lefts), hidden_from, sums)
    from_lefts, from_rights = send(h_lefts, Z_DOWN), send(h_rights, Z_UP)
    h_y, h_f = pass_on((h_y, h_f, from_lefts, from_rights, from_fl))
    from_y, from_f = send(h_y, Y_LO), send(h_f, Z_FAR)
    head_grad = finish((h_own, from_lefts, from_rights, from_f, from_y), SHORT)

    from_lefts, from_rights, from_fn = send(g_lefts, X_DOWN), send(g_rights, X_UP), send(after(g_far_near, from_fl), Y_HI)
    near_sum, far_sum = pass_on((after(g_near, h_y), g_far, from_lefts, from_rights, from_fn))
    from_far, from_near = send(far_sum, X_FAR), send(near_sum, Y_HI)
    return finish((after(g_own, head_grad), from_lefts, from_rights, from_far, from_near), SHORT), head_grad


def solution(mesh):
    in_specs = (
        P(("dp", "vocab"), None),
        P(("dp", "vocab"), None),
        P("vocab", None),
        P("vocab", None),
        P("dp"),
    )
    out_specs = (P(("dp", "vocab"), None), P(("vocab", "dp"), None))
    return jax.shard_map(
        on_device, mesh=mesh, in_specs=in_specs, out_specs=out_specs, check_vma=False
    )
```

```python
import functools

import jax
import jax.numpy as jnp
from jax import lax
from jax.experimental import pallas as pl
from jax.experimental.pallas import tpu as pltpu
from jax.sharding import PartitionSpec as P

BF16 = jnp.bfloat16
F32 = jnp.float32
AXES = ("dp", "vocab")

REL = ((0, 0), (0, 1), (-1, 0), (1, 0), (-1, 1), (1, 1), (2, 0), (2, 1))


def pairs(move):
    out = []
    for i in range(128):
        dp, v = i // 8, i % 8
        y_lo, z, core, x, y_hi = dp // 8, (dp // 2) % 4, dp % 2, v // 2, v % 2
        x, y, z, core = move(x, y_hi * 2 + y_lo, z, core)
        x, y, z = x % 4, y % 4, z % 4
        out.append((i, (((y % 2) * 4 + z) * 2 + core) * 8 + x * 2 + y // 2))
    return out


X_UP = pairs(lambda x, y, z, c: (x + 1, y, z, c))
X_DOWN = pairs(lambda x, y, z, c: (x - 1, y, z, c))
X_FAR = pairs(lambda x, y, z, c: (x + 2, y, z, c))
Y_HI = pairs(lambda x, y, z, c: (x, 3 - y, z, c))
Z_UP = pairs(lambda x, y, z, c: (x, y, z + 1, c))
Z_DOWN = pairs(lambda x, y, z, c: (x, y, z - 1, c))
Z_FAR = pairs(lambda x, y, z, c: (x, y, z + 2, c))
Y_LO = pairs(lambda x, y, z, c: (x, y ^ 1, z, c))
CORE = pairs(lambda x, y, z, c: (x, y, z, 1 - c))


def send(a, to):
    return lax.ppermute(a, AXES, to)


class Link:
    def __init__(self, to, ahead=2):
        self.to, self.ahead, self.sent = to, ahead, []

    def __call__(self, a):
        if len(self.sent) >= self.ahead:
            a = after(a, self.sent[-self.ahead])
        self.sent.append(send(a, self.to))
        return self.sent[-1]


def after(a, *others):
    return lax.optimization_barrier((a, *others))[0]


def params(mib):
    return pltpu.CompilerParams(vmem_limit_bytes=mib * 2**20)


LONG, SHORT = 20, 1


VMEM = pl.BlockSpec(memory_space=pltpu.VMEM)


def kernel_call(body, arrays, outs, scratch, mib, said=SHORT):
    return pl.pallas_call(
        body,
        in_specs=[VMEM] * len(arrays),
        out_specs=[VMEM] * len(outs),
        out_shape=[jax.ShapeDtypeStruct(shape, dtype) for shape, dtype in outs],
        scratch_shapes=[pltpu.VMEM(shape, dtype) for shape, dtype in scratch],
        compiler_params=params(mib),
        cost_estimate=pl.CostEstimate(flops=said * 10**9, bytes_accessed=said * 10**6, transcendentals=0),
    )(*arrays)


class Place:
    def __init__(self):
        dp, v = lax.axis_index("dp"), lax.axis_index("vocab")
        self.y_lo, self.z, self.core = lax.div(dp, 8), lax.rem(lax.div(dp, 2), 4), lax.rem(dp, 2)
        self.vocab, self.x, self.y_hi = v, lax.div(v, 2), lax.rem(v, 2)

    def owner(self, r):
        dx, dy = REL[r]
        return lax.rem(self.x + (dx + 4), 4) * 2 + lax.rem(self.y_hi + dy, 2)

    def chip(self, dz, dy):
        return lax.rem(self.y_lo + dy, 2) * 4 + lax.rem(self.z + (dz + 4), 4)


def block(r):
    return slice(r * 64, (r + 1) * 64)


def ids_kernel(own, near, ids):
    place = Place()
    half = lax.rem(lax.div(lax.broadcasted_iota(jnp.int32, (1, 512), 1), 64), 2)
    held = jnp.where(half == place.y_hi, own[...].reshape(1, 512), near[...].reshape(1, 512))
    for r in range(8):
        ids[:, block(r)] = sum(jnp.where(place.owner(r) == a, held[:, block(a)], 0) for a in range(8))


def fold(a):
    return jnp.sum(a.reshape(a.shape[0] // 8, 8, a.shape[1]), axis=0)


NT = (((1,), (1,)), ((), ()))
NN = (((1,), (0,)), ((), ()))
TILE = 576
WIDE = 512
STATS = (8, 512)


EARLY, LATE = slice(0, 256), slice(256, 512)


def put_blocks(blocks, hidden):
    for r, rows in enumerate(blocks):
        hidden[block(r), :] = rows[...]


def sums_of(out, ids, first):
    rows = lax.broadcasted_iota(jnp.int32, out.shape, 0) + first
    return fold(jnp.exp(out)), fold(jnp.where(rows == ids, out, 0.0))


def put_stats(stats, first, tokens, sums, picks):
    stats[first:first + 1, tokens] = jnp.sum(sums, axis=0, keepdims=True)
    stats[first + 1:first + 2, tokens] = jnp.sum(picks, axis=0, keepdims=True)


def advantage(total):
    norm = jnp.log(total[0:1, :])
    return (total[3:4, :] - jnp.log(total[2:3, :])) - (total[1:2, :] - norm), norm


def tiles(head):
    return [slice(j, j + TILE) for j in range(0, head.shape[0], TILE)]


def student_kernel(ids, head, *refs):
    blocks, (logits, hidden, stats) = refs[:8], refs[8:]
    put_blocks(blocks, hidden)
    first = Place().vocab * head.shape[0]
    sums = picks = 0.0
    for tile in tiles(head):
        out = lax.dot_general(head[tile, :], hidden[...], NT, preferred_element_type=F32)
        logits[tile, :] = out
        some, pick = sums_of(out, ids[...], first + tile.start)
        sums, picks = sums + some, picks + pick
    stats[...] = jnp.zeros_like(stats)
    put_stats(stats, 0, slice(0, 512), sums, picks)


def student_logits(ids, blocks, head):
    v, d = head.shape
    outs = [((v, 512), F32), ((512, d), BF16), (STATS, F32)]
    return kernel_call(student_kernel, (ids, head, *blocks), outs, [], 6, LONG)


def teacher_early_kernel(head, *refs):
    blocks, (logits, hidden) = refs[:4], refs[4:]
    put_blocks(blocks, hidden)
    for tile in tiles(head):
        logits[tile, :] = lax.dot_general(
            head[tile, hidden.shape[1]:], hidden[...], NT, preferred_element_type=F32
        )


def teacher_early(blocks, head):
    v, d = head.shape
    return kernel_call(teacher_early_kernel, (head, *blocks), [((v, 256), F32)], [((256, d // 2), BF16)], 6, LONG)[0]


def teacher_first_kernel(ids, student_stats, early, head, *refs):
    blocks, (logits, stats, hidden) = refs[:8], refs[8:]
    put_blocks(blocks, hidden)
    first = Place().vocab * head.shape[0]
    sums = picks = 0.0
    for tile in tiles(head):
        out = lax.dot_general(head[tile, 0:hidden.shape[1]], hidden[...], NT, preferred_element_type=F32)
        logits[tile, :] = out[:, LATE]
        some, pick = sums_of(out[:, EARLY] + early[tile, :], ids[:, EARLY], first + tile.start)
        sums, picks = sums + some, picks + pick
    stats[...] = student_stats[...]
    put_stats(stats, 2, EARLY, sums, picks)


def teacher_first(ids, student_stats, early, blocks, head):
    v, d = head.shape
    arrays = (ids, student_stats, early, head, *blocks)
    return kernel_call(teacher_first_kernel, arrays, [((v, 256), F32), (STATS, F32)], [((512, d // 2), BF16)], 8, LONG)


def teacher_second_kernel(ids, first_stats, head, logits, *refs):
    blocks, (stats, hidden) = refs[:4], refs[4:]
    put_blocks(blocks, hidden)
    first = Place().vocab * head.shape[0]
    sums = picks = 0.0
    for tile in tiles(head):
        out = logits[tile, :] + lax.dot_general(
            head[tile, hidden.shape[1]:], hidden[...], NT, preferred_element_type=F32
        )
        some, pick = sums_of(out, ids[:, LATE], first + tile.start)
        sums, picks = sums + some, picks + pick
    stats[...] = first_stats[...]
    put_stats(stats, 2, LATE, sums, picks)


def teacher_second(ids, stats, blocks, head, logits):
    scratch = [((256, head.shape[1] // 2), BF16)]
    return kernel_call(teacher_second_kernel, (ids, stats, head, logits, *blocks), [(STATS, F32)], scratch, 6, LONG)[0]


def hidden_kernel(groups, places, ids, total, logits, head, *refs):
    outs, grad_t = refs[:-1], refs[-1]
    first = Place().vocab * head.shape[0]
    adv, norm = advantage(total)
    for i, start in enumerate(groups):
        tokens = slice(start, start + 128)
        for k in range(0, head.shape[0], 128):
            rows = lax.broadcasted_iota(jnp.int32, (128, 128), 0) + (first + k)
            onehot = jnp.where(rows == ids[:, tokens], 1.0, 0.0)
            part = adv[:, tokens] * (jnp.exp(logits[k:k + 128, tokens] - norm[:, tokens]) - onehot)
            grad_t[i * 128:(i + 1) * 128, k:k + 128] = part.T.astype(BF16)
    for j in range(0, head.shape[1], WIDE):
        tile = slice(j, j + WIDE)
        product = lax.dot_general(grad_t[...], head[:, tile], NN, preferred_element_type=F32)
        for r, (out, row) in enumerate(places):
            outs[out][row:row + 64, tile] = product[block(r), :].astype(outs[out].dtype)


def hidden_parts(ids, total, logits, head, groups, places, outs, said):
    v, d = head.shape
    outs = [((n, d), t) for n, t in outs]
    body = functools.partial(hidden_kernel, groups, places)
    return kernel_call(body, (ids, total, logits, head), outs, [((256, v), BF16)], 6, said)


def hidden_outer(*arrays):
    places = ((0, 0), (1, 0), (0, 64), (1, 64))
    return hidden_parts(*arrays, (128, 256), places, ((128, BF16),) * 2, LONG)


def hidden_inner(*arrays):
    places = ((0, 0), (1, 0), (2, 0), (3, 0))
    return hidden_parts(*arrays, (0, 384), places, ((64, F32),) * 3 + ((64, BF16),), SHORT)


CHIPS = ((-1, 0), (-1, 1), (1, 0), (1, 1), (2, 1), (2, 0), (0, 1), (0, 0))


def grad_kernel(ids, total, logits, mine, other, mine_f, other_f):
    place = Place()
    adv, norm = advantage(total)
    for r, chip in enumerate(CHIPS):
        for out, core in ((mine_f, place.core), (other_f, 1 - place.core)):
            start = pl.multiple_of(place.chip(*chip) * 144 + core * 72, 8)
            rows = lax.broadcasted_iota(jnp.int32, (72, 512), 0) + (place.vocab * logits.shape[0] + start)
            onehot = jnp.where(rows == ids[...], 1.0, 0.0)
            probs = jnp.exp(logits[pl.ds(start, 72), :] - norm)
            out[r * 72:(r + 1) * 72, :] = adv * (probs - onehot)
    mine[...] = mine_f[...].astype(BF16)
    other[...] = other_f[...].astype(BF16)


def logit_grads(ids, total, logits):
    half = logits.shape[0] // 2
    outs = [((half, 512), BF16)] * 2
    return kernel_call(grad_kernel, (ids, total, logits), outs, [((half, 512), F32)] * 2, 5, LONG)


def head_own_kernel(grad, hidden, out):
    for j in range(0, hidden.shape[1], WIDE):
        tile = slice(j, j + WIDE)
        out[:, tile] = lax.dot_general(grad[...], hidden[:, tile], NN, preferred_element_type=F32)


def head_own(grad, hidden):
    outs = [((grad.shape[0], hidden.shape[1]), F32)]
    return kernel_call(head_own_kernel, (grad, hidden), outs, [], 4)[0]


def head_kernel(first, grad, hidden, own, *outs):
    n = sum(out.shape[0] for out in outs)
    rows = slice(first, first + n)
    for j in range(0, hidden.shape[1], WIDE):
        tile = slice(j, j + WIDE)
        product = own[rows, tile] + lax.dot_general(grad[rows, :], hidden[:, tile], NN, preferred_element_type=F32)
        start = 0
        for out in outs:
            out[:, tile] = product[start:start + out.shape[0], :].astype(out.dtype)
            start += out.shape[0]


def head_parts(first, outs, grad, hidden, own):
    outs = [((n, hidden.shape[1]), t) for n, t in outs]
    return kernel_call(functools.partial(head_kernel, first), (grad, hidden, own), outs, [], 4)


def pass_on_kernel(near, far, lefts, rights, far_near, near_out, far_out):
    n = near.shape[0]
    near_out[...] = (near[...] + lefts[n:, :].astype(F32) + rights[n:, :].astype(F32)).astype(near_out.dtype)
    far_out[...] = (far[...] + far_near[...].astype(F32)).astype(far_out.dtype)


def pass_on(pieces):
    return kernel_call(pass_on_kernel, pieces, [(pieces[0].shape, BF16)] * 2, [], 4, LONG)


def finish_kernel(own, lefts, rights, far, near, out):
    n = out.shape[0]
    total = own[...] + lefts[0:n, :].astype(F32) + rights[0:n, :].astype(F32)
    out[...] = (total + far[...].astype(F32) + near[...].astype(F32)).astype(out.dtype)


def finish(pieces, said):
    return kernel_call(finish_kernel, pieces, [(pieces[0].shape, BF16)], [], 4, said)[0]


def merge_kernel(shifts, *refs):
    arrays, out = refs[:-1], refs[-1]
    for r, (dx, dy) in enumerate(REL):
        total = 0.0
        for (sx, sy), a in zip(shifts, arrays):
            there = [i for i, (ox, oy) in enumerate(REL) if (ox + sx - dx) % 4 == 0 and (oy + sy - dy) % 2 == 0][0]
            total += a[:, block(there)]
        out[:, block(r)] = total


def merge(shifts, arrays):
    return kernel_call(functools.partial(merge_kernel, shifts), arrays, [(STATS, F32)], [], 2)[0]


def group_sum(a):
    around = merge(((0, 0), (-1, 0), (1, 0), (2, 0)), (a, send(a, X_UP), send(a, X_DOWN), send(a, X_FAR)))
    return merge(((0, 0), (0, 1)), (around, send(around, Y_HI)))


def on_device(student_hidden, teacher_hidden, student_head, teacher_head, sampled_ids):
    up, down, over = Link(X_UP), Link(X_DOWN), Link(Y_HI)
    half = teacher_hidden.shape[1] // 2
    t_a, t_b = teacher_hidden[:, :half], teacher_hidden[:, half:]
    t_b0 = t_b
    left = up(student_hidden)
    right = down(student_hidden)
    near = over(student_hidden)
    ids_near = send(sampled_ids, Y_HI)
    ids = kernel_call(ids_kernel, (sampled_ids, ids_near), [((1, 512), jnp.int32)], [], 1, LONG)[0]
    t_b0, t_b = t_b, after(t_b, ids)
    l_b = up(t_b)
    r_a = down(t_a)
    near_a = over(after(t_a, ids_near))
    far = up(left)
    right_near = down(near)
    near_b = over(t_b0)
    l_a = up(t_a)
    f_a = down(r_a)
    left_near = over(left)
    f_b = up(l_b)
    r_b = down(t_b)
    far_near = over(far)
    ln_a = up(near_a)
    rn_a = down(near_a)
    fn_a = over(f_a)

    blocks = (student_hidden, near, left, right, left_near, right_near, far, far_near)
    logits, hidden, student_stats = student_logits(after(ids, rn_a), blocks, student_head)
    fn_b = over(f_b)
    ln_b = up(near_b)
    rn_b = down(near_b)

    hidden_from = send(hidden, CORE)
    early = teacher_early((t_b, near_b, l_b, r_b), teacher_head)
    blocks = (t_a, near_a, l_a, r_a, ln_a, rn_a, f_a, fn_a)
    teacher_logits, stats = teacher_first(ids, student_stats, early, blocks, teacher_head)
    total = group_sum(teacher_second(ids, stats, (ln_b, rn_b, f_b, fn_b), teacher_head, teacher_logits))

    mine, other = logit_grads(ids, total, logits)
    grad_from, sums = send(other, CORE), head_own(mine, hidden)
    h_lefts, h_rights, h_fl = head_parts(0, ((144, BF16), (144, BF16), (72, BF16)), grad_from, hidden_from, sums)
    g_lefts, g_rights = hidden_outer(ids, after(total, h_fl), logits, student_head)
    from_fl = send(h_fl, Y_LO)
    g_own, g_near, g_far, g_far_near = hidden_inner(ids, after(total, from_fl), logits, student_head)
    h_f, h_y, h_own = head_parts(360, ((72, F32),) * 3, after(grad_from, g_lefts), hidden_from, sums)
    from_lefts, from_rights = send(h_lefts, Z_DOWN), send(h_rights, Z_UP)
    h_y, h_f = pass_on((h_y, h_f, from_lefts, from_rights, from_fl))
    from_y, from_f = send(h_y, Y_LO), send(h_f, Z_FAR)
    head_grad = finish((h_own, from_lefts, from_rights, from_f, from_y), SHORT)

    from_lefts, from_rights, from_fn = send(g_lefts, X_DOWN), send(g_rights, X_UP), send(after(g_far_near, from_fl), Y_HI)
    near_sum, far_sum = pass_on((after(g_near, h_y), g_far, from_lefts, from_rights, from_fn))
    from_far, from_near = send(far_sum, X_FAR), send(near_sum, Y_HI)
    return finish((after(g_own, head_grad), from_lefts, from_rights, from_far, from_near), SHORT), head_grad


def solution(mesh):
    in_specs = (
        P(("dp", "vocab"), None),
        P(("dp", "vocab"), None),
        P("vocab", None),
        P("vocab", None),
        P("dp"),
    )
    out_specs = (P(("dp", "vocab"), None), P(("vocab", "dp"), None))
    return jax.shard_map(
        on_device, mesh=mesh, in_specs=in_specs, out_specs=out_specs, check_vma=False
    )
```
